512 devices in a mesh: pair: 256 (over z, y, x), tm: 2 (over core).
Axes of the slice: x: 4, y: 8, z: 8, core: 2. Of those that a mesh axis runs over, the one named last changes fastest.
Arguments:
- traces: float32 [8192, 2, 4096], P('pair', 'tm'), may hold values from -600 to 600, as said below
- pair_list: int32 [8192, 2], P('pair'), may hold values from 0 to 8191, as said below
- live_pairs: int32 [256], P('pair'), may hold values from 4 to 32, as said below
Outputs:
- correlations: float32 [8192, 2048], P(('pair', 'tm'))
The draws below stay inside these ranges and needn't reach their ends.
Inputs may be any that keep to these rules, and one draw needn't show every extreme that they name: `pair_list`: rows j * 32 to (j + 1) * 32 - 1 have their first channel in [j * 32, (j + 1) * 32); the second channel differs from the first by at most 32, and by exactly 32 in some row of every draw. The first live_pairs[j] slots of owner j are live; some owner has all 32 live. `traces`: records in arbitrary units.
All inputs are finite; a program needn't handle non-finite values.
Results may differ from the reference program's by a relative error of at most 0.0085.
Values may be sent and summed in bfloat16 or wider, within the bound.
A program may use at most 64 MiB of HBM per device.

```python
import math
import jax
import jax.numpy as jnp
from jax import lax

NT = 4096
FB = 2048
NLAG = 2048
HALF = 64
CH_DEV = 32
PAIR_DEV = 32
CHANNELS = 8192
SEGMENTS = 2
PAIRS = 8192
REACH = 32
OWNERS = 256
N_PAIR = 256


def draw_traces(key, part):
    key = jax.random.fold_in(key, 11)
    subkeys = jax.random.split(key, 5)
    sample_times = jnp.arange(NT).astype(jnp.float32)
    random_part = jnp.clip(jax.random.normal(subkeys[0], (CHANNELS, SEGMENTS, NT), jnp.float32), -6.0, 6.0)
    log_top = math.log(10.0)
    channel_gain = jnp.exp(jax.random.uniform(subkeys[1], (CHANNELS, SEGMENTS, 1), jnp.float32, 0.0, log_top))
    signal = random_part
    for harmonic in range(6):
        frequency = jax.random.uniform(jax.random.fold_in(subkeys[2], harmonic), (CHANNELS, 1, 1), jnp.float32, 0.01, 0.45)
        amplitude = jax.random.uniform(jax.random.fold_in(subkeys[3], harmonic), (CHANNELS, 1, 1), jnp.float32, 0.3, 2.0)
        phase_shift = jax.random.uniform(jax.random.fold_in(subkeys[4], harmonic), (CHANNELS, SEGMENTS, 1), jnp.float32, -math.pi, math.pi)
        signal = signal + amplitude * jnp.sin(2.0 * math.pi * frequency * sample_times + phase_shift)
    return channel_gain * signal


def draw_pair_list(key, part):
    key = jax.random.fold_in(key, 21)
    first_key, second_key = jax.random.split(key)
    slot_index = jnp.arange(PAIRS, dtype=jnp.int32)
    owner = slot_index // PAIR_DEV
    within = slot_index % PAIR_DEV
    first_channel = owner * CH_DEV + jax.random.randint(first_key, (PAIRS,), 0, CH_DEV, dtype=jnp.int32)
    offsets = jax.random.randint(second_key, (PAIRS,), -REACH, REACH + 1, dtype=jnp.int32)
    offsets = jnp.where(within == 0, REACH, offsets)
    second_channel = first_channel + offsets
    outside = (second_channel < 0) | (second_channel >= CHANNELS)
    second_channel = jnp.where(outside, first_channel - offsets, second_channel)
    return jnp.stack([first_channel, second_channel], axis=1).astype(jnp.int32)


def draw_live_pairs(key, part):
    key = jax.random.fold_in(key, 31)
    shift_key, full_key = jax.random.split(key)
    halvings = jax.random.randint(shift_key, (OWNERS,), 0, 4, dtype=jnp.int32)
    counted = jnp.right_shift(jnp.full((OWNERS,), PAIR_DEV, jnp.int32), halvings)
    chosen = jax.random.randint(full_key, (), 0, OWNERS, dtype=jnp.int32)
    return jnp.where(jnp.arange(OWNERS, dtype=jnp.int32) == chosen, PAIR_DEV, counted).astype(jnp.int32)


def setup_inputs(seed: int = 0) -> dict:
    streams_of = jax.random.split(jax.random.key(seed), 4)
    traces = draw_traces(jax.random.fold_in(streams_of[3], 71), 0)
    pair_list = draw_pair_list(jax.random.fold_in(streams_of[3], 71), 0)
    live_pairs = draw_live_pairs(jax.random.fold_in(streams_of[3], 71), 0)
    return {"traces": traces, "pair_list": pair_list, "live_pairs": live_pairs}


TWO_PI = 2.0 * math.pi
EPSILON = 1e-06

def lag_table(begin, width, scale):
    frequency = jnp.arange(1, FB + 1).astype(jnp.int32)
    shifts = ((jnp.arange(width).astype(jnp.int32) + begin - NLAG // 2) % NT).astype(jnp.int32)
    phases = frequency[:, None] * shifts[None, :] % NT
    angles = TWO_PI * phases.astype(jnp.float32) / NT
    return jnp.concatenate([jnp.cos(angles), -jnp.sin(angles)], axis=0) * scale

def whiten_all(traces):
    spectrum = jnp.fft.rfft(traces, axis=-1)[..., 1:FB + 1]
    real_part = jnp.real(spectrum).astype(jnp.float32)
    imag_part = jnp.imag(spectrum).astype(jnp.float32)
    magnitude = jnp.sqrt(real_part * real_part + imag_part * imag_part)
    padded = jnp.pad(magnitude, ((0, 0), (0, 0), (HALF + 1, HALF)))
    running = jnp.cumsum(padded, axis=-1)
    window_sum = running[..., 2 * HALF + 1:2 * HALF + 1 + FB] - running[..., :FB]
    centre = jnp.arange(FB)
    counted = jnp.minimum(centre + HALF, FB - 1) - jnp.maximum(centre - HALF, 0) + 1
    level_mean = window_sum / counted.astype(jnp.float32)
    inverse = 1.0 / (level_mean + EPSILON)
    return jnp.concatenate([real_part * inverse, imag_part * inverse], axis=-1).astype(jnp.bfloat16)

def reference(traces, pair_list, live_pairs):
    whitened = whiten_all(traces)
    grouped = pair_list.reshape(N_PAIR, PAIR_DEV, 2)

    def cross_block(members):
        first_rows = whitened[members[:, 0]].astype(jnp.float32)
        second_rows = whitened[members[:, 1]].astype(jnp.float32)
        real_a, imag_a = (first_rows[..., :FB], first_rows[..., FB:])
        real_b, imag_b = (second_rows[..., :FB], second_rows[..., FB:])
        cross_real = lax.optimization_barrier(jnp.sum(real_a * real_b + imag_a * imag_b, axis=1))
        cross_imag = lax.optimization_barrier(jnp.sum(imag_a * real_b - real_a * imag_b, axis=1))
        return jnp.concatenate([cross_real, cross_imag], axis=-1)
    cross_spec = lax.map(cross_block, grouped).reshape(PAIRS, NT)
    weights = lag_table(0, NLAG, 1.0 / math.sqrt(FB * SEGMENTS))
    product = jnp.dot(cross_spec, weights, precision=lax.Precision.HIGHEST, preferred_element_type=jnp.float32)
    row_index = jnp.arange(PAIRS).astype(jnp.int32)
    owner_live = live_pairs[row_index // PAIR_DEV]
    wanted = row_index % PAIR_DEV < owner_live
    return jnp.where(wanted[:, None], product, 0.0)
```

```python
import functools
import math

import jax
import jax.numpy as jnp
import numpy as np
from jax import lax
from jax.experimental import pallas as pl
from jax.experimental.pallas import tpu as pltpu
from jax.sharding import PartitionSpec as P

NT = 4096
FB = 2048
NLAG = 2048
HALF = 64
EPSILON = 1e-06

RADIX = 32
LANES = 128
SLABS = 16
CHUNK = 8
MESH = pl.DeviceIdType.MESH


def split(table):
    high = table.astype(jnp.bfloat16)
    low = (table - high.astype(np.float64)).astype(jnp.bfloat16)
    return np.stack([high, low])


def tables():
    n0 = np.arange(LANES)
    k2 = np.arange(LANES // 2)
    q = np.concatenate([k2, LANES - 1 - k2])
    sign = np.concatenate([np.ones(LANES // 2), -np.ones(LANES // 2)])
    angle = 2.0 * math.pi * (n0[:, None] * q[None, :] % LANES) / LANES
    cos, sin = np.cos(angle), np.sin(angle)
    forward = np.block([[cos, -sin * sign], [sin, cos * sign]])
    inverse = np.block([[cos.T, sin.T], [-sin.T * sign[:, None], cos.T * sign[:, None]]])
    inverse = inverse / 64.0
    s = np.arange(SLABS + 1)
    twist = 2.0 * math.pi * (s[:, None] * n0[None, :]) / NT
    k1 = np.stack([np.where(s[:16] == 0, 16, s[:16]), 32 - s[:16]], axis=1)
    index = (k1[:, :, None] - 1 + RADIX * k2[None, None, :]).reshape(SLABS, LANES)
    counted = np.minimum(index + HALF, FB - 1) - np.maximum(index - HALF, 0) + 1
    small = np.zeros((56, LANES))
    small[0:17] = np.cos(twist)
    small[17:34] = np.sin(twist)
    small[34:50] = counted
    return split(forward), split(inverse), small.astype(np.float32)


def scaled(value, factor):
    return value if factor == 1.0 else -value if factor == -1.0 else value * factor


def real_dft(values):
    count = len(values)
    if count == 2:
        return [(values[0] + values[1], None), (values[0] - values[1], None)]
    even, odd = real_dft(values[0::2]), real_dft(values[1::2])
    quarter = count // 4
    bins = [None] * (count // 2 + 1)
    bins[0] = (even[0][0] + odd[0][0], None)
    bins[count // 2] = (even[0][0] - odd[0][0], None)
    for k in range(1, quarter):
        c, s = math.cos(2.0 * math.pi * k / count), math.sin(2.0 * math.pi * k / count)
        (er, ei), (pr, pi) = even[k], odd[k]
        if 8 * k == count:
            tr, ti = (pr + pi) * c, (pi - pr) * c
        else:
            tr, ti = pr * c + pi * s, pi * c - pr * s
        bins[k] = (er + tr, ei + ti)
        bins[count // 2 - k] = (er - tr, ti - ei)
    er, pr = even[quarter][0], odd[quarter][0]
    bins[quarter] = (er, -pr)
    return bins


def real_sum(bins, count, wanted):
    if count == 2:
        (ar, _), (br, _) = bins
        return {l: ar + br if l == 0 else ar - br for l in wanted}
    quarter = count // 4
    even, odd = [], []
    for s in range(quarter):
        (ar, ai), (br, bi) = bins[s], bins[count // 2 - s]
        if s == 0:
            even.append((ar + br, None))
            odd.append((ar - br, None))
            continue
        even.append((ar + br, ai - bi))
        dr, di = ar - br, ai + bi
        c, n = math.cos(2.0 * math.pi * s / count), math.sin(2.0 * math.pi * s / count)
        if 8 * s == count:
            odd.append(((dr - di) * c, (dr + di) * c))
        else:
            odd.append((dr * c - di * n, dr * n + di * c))
    mr, mi = bins[quarter]
    even.append((mr, None))
    odd.append((-mi, None))
    half = count // 2
    from_even = real_sum(even, half, sorted({l // 2 for l in wanted if l % 2 == 0}))
    from_odd = real_sum(odd, half, sorted({l // 2 for l in wanted if l % 2 == 1}))
    return {l: (from_odd if l % 2 else from_even)[l // 2] for l in wanted}


def halves(value):
    high = value.astype(jnp.bfloat16)
    return high, (value - high.astype(jnp.float32)).astype(jnp.bfloat16)


def dot3(value, table):
    high, low = halves(value)
    dot = functools.partial(jnp.dot, preferred_element_type=jnp.float32)
    return dot(high, table[0]) + (dot(low, table[0]) + dot(high, table[1]))


def spectra(x_ref, small, forward, base):
    values = [x_ref[pl.ds(base * RADIX + n1, CHUNK, stride=RADIX), :] for n1 in range(RADIX)]
    turned_re, turned_im = [], []
    for s, (re, im) in enumerate(real_dft(values)):
        c, n = small[s : s + 1, :], small[17 + s : 18 + s, :]
        if s == 0:
            turned_re.append(re)
            turned_im.append(jnp.zeros_like(re))
        elif im is None:
            turned_re.append(re * c)
            turned_im.append(-re * n)
        else:
            turned_re.append(re * c + im * n)
            turned_im.append(im * c - re * n)
    rows = jnp.concatenate(
        [jnp.concatenate(turned_re, axis=0), jnp.concatenate(turned_im, axis=0)], axis=1
    )
    final = dot3(rows, forward)
    re = [final[s * CHUNK : (s + 1) * CHUNK, :LANES] for s in range(17)]
    im = [final[s * CHUNK : (s + 1) * CHUNK, LANES:] for s in range(17)]
    first = lax.broadcasted_iota(jnp.int32, (CHUNK, LANES), 1) < LANES // 2
    re[0] = jnp.where(first, re[16], re[0])
    im[0] = jnp.where(first, im[16], im[0])
    return re[:16], im[:16]


def whitened(re, im, small):
    lane = lax.broadcasted_iota(jnp.int32, (CHUNK, LANES), 1)
    first = lane < LANES // 2
    k2 = lane % (LANES // 2)
    size = [jnp.sqrt(a * a + b * b) for a, b in zip(re, im)]
    running = [jnp.zeros_like(size[0])]
    for s in range(1, SLABS):
        running.append(running[-1] + size[s])
    total = running[15] + size[0]
    total = total + pltpu.roll(total, LANES // 2, 1)
    centre = (
        total
        + jnp.where(k2 >= 1, pltpu.roll(total, 1, 1), 0.0)
        + jnp.where(k2 <= 62, pltpu.roll(total, LANES - 1, 1), 0.0)
    )
    before = pltpu.roll(running[15] + size[0], LANES // 2, 1) + running[15]
    out = []
    for s in range(SLABS):
        if s == 0:
            prefix = jnp.where(first, running[15] + size[0], total)
            suffix = jnp.where(first, total - running[15], size[0])
        else:
            prefix = jnp.where(first, running[s], before - running[s - 1])
            suffix = jnp.where(first, total - running[s - 1], running[s] + size[0])
        window = (
            centre
            + jnp.where(k2 >= 2, pltpu.roll(suffix, 2, 1), 0.0)
            + jnp.where(k2 <= 61, pltpu.roll(prefix, LANES - 2, 1), 0.0)
        )
        counted = small[34 + s : 35 + s, :]
        scale = counted / (window + EPSILON * counted)
        out.append((re[s] * scale, im[s] * scale))
    return out


def kernel(
    rows,
    traces,
    pair_list,
    live,
    forward_hbm,
    inverse_hbm,
    small_hbm,
    out_ref,
    x_ref,
    forward,
    inverse,
    small,
    turn,
    ext,
    cross_out,
    cross_own,
    cross_in,
    load_sem,
    table_sem,
    send_sem,
    recv_sem,
    swap_sem,
):
    me = lax.axis_index("pair")
    core = lax.axis_index("tm")
    count = lax.axis_size("pair")
    chunks = rows // CHUNK
    loads = [
        pltpu.make_async_copy(
            traces.at[pl.ds(i * CHUNK * RADIX, CHUNK * RADIX)],
            x_ref.at[pl.ds(i * CHUNK * RADIX, CHUNK * RADIX)],
            load_sem.at[i],
        )
        for i in range(chunks)
    ]
    table_loads = [
        pltpu.make_async_copy(src, dst, table_sem.at[i])
        for i, (src, dst) in enumerate(
            [(small_hbm, small), (forward_hbm, forward), (inverse_hbm, inverse)]
        )
    ]
    loads[0].start()
    table_loads[0].start()
    table_loads[1].start()
    for copy in loads[1:]:
        copy.start()
    table_loads[2].start()

    before, after = lax.rem(me + count - 1, count), lax.rem(me + 1, count)
    barrier = pltpu.get_barrier_semaphore()
    for target in ((before, core), (after, core), (me, 1 - core)):
        pl.semaphore_signal(barrier, inc=1, device_id=target, device_id_type=MESH)

    sends = []
    for i in range(chunks):
        loads[i].wait()
        if i == 0:
            table_loads[0].wait()
            table_loads[1].wait()
        re, im = spectra(x_ref, small, forward, i * CHUNK)
        for s, (a, b) in enumerate(whitened(re, im, small)):
            place = i * CHUNK * 32 + s // 8 * 16 + s % 8
            turn[pl.ds(place, CHUNK, stride=32), :] = a
            turn[pl.ds(place + 8, CHUNK, stride=32), :] = b
        own = pl.ds(rows + i * CHUNK, CHUNK)
        part = turn[pl.ds(i * CHUNK * 32, CHUNK * 32), :].reshape(CHUNK, 2, 16, LANES)
        ext[own] = part.astype(jnp.bfloat16)
        if i == 0:
            pl.semaphore_wait(barrier, 3)
        for way, (target, place) in enumerate(((before, 2 * rows), (after, 0))):
            copy = pltpu.make_async_remote_copy(
                src_ref=ext.at[own],
                dst_ref=ext.at[pl.ds(place + i * CHUNK, CHUNK)],
                send_sem=send_sem.at[way, i],
                recv_sem=recv_sem.at[way, i],
                device_id=(target, core),
                device_id_type=MESH,
            )
            copy.start()
            sends.append(copy)
    for copy in sends:
        copy.wait()

    anchor = me * rows - rows
    kept = rows // 2

    def cross(into, slot, i):
        first = jnp.clip(pair_list[slot, 0] - anchor, 0, 3 * rows - 1)
        second = jnp.clip(pair_list[slot, 1] - anchor, 0, 3 * rows - 1)
        for g in range(2):
            a = ext[first, g].astype(jnp.float32)
            b = ext[second, g].astype(jnp.float32)
            ar, ai, br, bi = a[:8], a[8:], b[:8], b[8:]
            place = pl.ds(g * 8 * kept + i, 8, stride=kept)
            into[0, place, :] = ar * br + ai * bi
            into[1, place, :] = ai * br - ar * bi

    for i in range(kept):
        cross(cross_out, (1 - core) * kept + i, i)
    swap = pltpu.make_async_remote_copy(
        src_ref=cross_out,
        dst_ref=cross_in,
        send_sem=swap_sem.at[0],
        recv_sem=swap_sem.at[1],
        device_id=(me, 1 - core),
        device_id_type=MESH,
    )
    swap.start()
    for i in range(kept):
        cross(cross_own, core * kept + i, i)
    table_loads[2].wait()
    swap.wait()

    both = jnp.concatenate(
        [cross_own[0] + cross_in[0], cross_own[1] + cross_in[1]], axis=1
    )
    lane = lax.broadcasted_iota(jnp.int32, (kept, 2 * LANES), 1) % LANES
    zeroth = both[:kept]
    spread = jnp.concatenate(
        [
            jnp.where(lane < LANES // 2, 0.0, zeroth),
            both[kept:],
            jnp.where(lane < LANES // 2, zeroth, 0.0),
        ],
        axis=0,
    )
    lags = dot3(spread, inverse)
    for part in range(kept // 8):
        bins = []
        for s in range(17):
            place = slice(s * kept + part * 8, s * kept + part * 8 + 8)
            vr, vi = lags[place, :LANES], lags[place, LANES:]
            c, n = small[s : s + 1, :], small[17 + s : 18 + s, :]
            if s == 0:
                bins.append((vr, None))
            elif s == 16:
                bins.append((vr * c - vi * n, None))
            else:
                bins.append((vr * c - vi * n, vr * n + vi * c))
        blocks = real_sum(bins, RADIX, [l1 % RADIX for l1 in range(-8, 8)])
        slot = core * kept + part * 8 + lax.broadcasted_iota(jnp.int32, (8, LANES), 0)
        wanted = slot < live[0]
        for l1 in range(-8, 8):
            out_ref[part * 8 : part * 8 + 8, (l1 + 8) * LANES : (l1 + 9) * LANES] = jnp.where(
                wanted, blocks[l1 % RADIX], 0.0
            )


def shards(traces, pair_list, live_pairs):
    rows = traces.shape[0]
    kept = rows // 2
    chunks = rows // CHUNK
    forward, inverse, small = tables()
    any_space = pl.BlockSpec(memory_space=pl.ANY)
    scalars = pl.BlockSpec(memory_space=pltpu.SMEM)
    f32, bf16 = jnp.float32, jnp.bfloat16
    return pl.pallas_call(
        functools.partial(kernel, rows),
        out_shape=jax.ShapeDtypeStruct((kept, NLAG), f32),
        in_specs=[any_space, scalars, scalars, any_space, any_space, any_space],
        out_specs=pl.BlockSpec(memory_space=pltpu.VMEM),
        scratch_shapes=[
            pltpu.VMEM((rows * RADIX, LANES), f32),
            pltpu.VMEM(forward.shape, bf16),
            pltpu.VMEM(inverse.shape, bf16),
            pltpu.VMEM(small.shape, f32),
            pltpu.VMEM((rows * 32, LANES), f32),
            pltpu.VMEM((3 * rows, 2, 16, LANES), bf16),
            pltpu.VMEM((2, SLABS * kept, LANES), f32),
            pltpu.VMEM((2, SLABS * kept, LANES), f32),
            pltpu.VMEM((2, SLABS * kept, LANES), f32),
            pltpu.SemaphoreType.DMA((chunks,)),
            pltpu.SemaphoreType.DMA((3,)),
            pltpu.SemaphoreType.DMA((2, chunks)),
            pltpu.SemaphoreType.DMA((2, chunks)),
            pltpu.SemaphoreType.DMA((2,)),
        ],
        compiler_params=pltpu.CompilerParams(
            collective_id=0, has_side_effects=True, vmem_limit_bytes=32 * 1024 * 1024
        ),
        name="correlate",
    )(
        traces.reshape(rows * RADIX, LANES),
        pair_list,
        live_pairs,
        jnp.asarray(forward),
        jnp.asarray(inverse),
        jnp.asarray(small),
    )


def solution(mesh):
    placed = (P("pair", "tm", None), P("pair", None), P("pair"))
    return jax.shard_map(
        shards, mesh=mesh, in_specs=placed, out_specs=P(("pair", "tm"), None), check_vma=False
    )
```

```python
import functools
import math

import jax
import jax.numpy as jnp
import numpy as np
from jax import lax
from jax.experimental import pallas as pl
from jax.experimental.pallas import tpu as pltpu
from jax.sharding import PartitionSpec as P

NT = 4096
FB = 2048
NLAG = 2048
HALF = 64
EPSILON = 1e-06

RADIX = 32
LANES = 128
SLABS = 16
CHUNK = 8
MESH = pl.DeviceIdType.MESH


def split(table):
    high = table.astype(jnp.bfloat16)
    low = (table - high.astype(np.float64)).astype(jnp.bfloat16)
    return np.stack([high, low])


def tables():
    n0 = np.arange(LANES)
    k2 = np.arange(LANES // 2)
    q = np.concatenate([k2, LANES - 1 - k2])
    sign = np.concatenate([np.ones(LANES // 2), -np.ones(LANES // 2)])
    angle = 2.0 * math.pi * (n0[:, None] * q[None, :] % LANES) / LANES
    cos, sin = np.cos(angle), np.sin(angle)
    forward = np.block([[cos, -sin * sign], [sin, cos * sign]])
    inverse = np.block([[cos.T, sin.T], [-sin.T * sign[:, None], cos.T * sign[:, None]]])
    inverse = inverse / 64.0
    s = np.arange(SLABS + 1)
    twist = 2.0 * math.pi * (s[:, None] * n0[None, :]) / NT
    k1 = np.stack([np.where(s[:16] == 0, 16, s[:16]), 32 - s[:16]], axis=1)
    index = (k1[:, :, None] - 1 + RADIX * k2[None, None, :]).reshape(SLABS, LANES)
    counted = np.minimum(index + HALF, FB - 1) - np.maximum(index - HALF, 0) + 1
    small = np.zeros((56, LANES))
    small[0:17] = np.cos(twist)
    small[17:34] = np.sin(twist)
    small[34:50] = counted
    return split(forward), split(inverse), small.astype(np.float32)


def scaled(value, factor):
    return value if factor == 1.0 else -value if factor == -1.0 else value * factor


def real_dft(values):
    count = len(values)
    if count == 2:
        return [(values[0] + values[1], None), (values[0] - values[1], None)]
    even, odd = real_dft(values[0::2]), real_dft(values[1::2])
    quarter = count // 4
    bins = [None] * (count // 2 + 1)
    bins[0] = (even[0][0] + odd[0][0], None)
    bins[count // 2] = (even[0][0] - odd[0][0], None)
    for k in range(1, quarter):
        c, s = math.cos(2.0 * math.pi * k / count), math.sin(2.0 * math.pi * k / count)
        (er, ei), (pr, pi) = even[k], odd[k]
        if 8 * k == count:
            tr, ti = (pr + pi) * c, (pi - pr) * c
        else:
            tr, ti = pr * c + pi * s, pi * c - pr * s
        bins[k] = (er + tr, ei + ti)
        bins[count // 2 - k] = (er - tr, ti - ei)
    er, pr = even[quarter][0], odd[quarter][0]
    bins[quarter] = (er, -pr)
    return bins


def real_sum(bins, count, wanted):
    if count == 2:
        (ar, _), (br, _) = bins
        return {l: ar + br if l == 0 else ar - br for l in wanted}
    quarter = count // 4
    even, odd = [], []
    for s in range(quarter):
        (ar, ai), (br, bi) = bins[s], bins[count // 2 - s]
        if s == 0:
            even.append((ar + br, None))
            odd.append((ar - br, None))
            continue
        even.append((ar + br, ai - bi))
        dr, di = ar - br, ai + bi
        c, n = math.cos(2.0 * math.pi * s / count), math.sin(2.0 * math.pi * s / count)
        if 8 * s == count:
            odd.append(((dr - di) * c, (dr + di) * c))
        else:
            odd.append((dr * c - di * n, dr * n + di * c))
    mr, mi = bins[quarter]
    even.append((mr, None))
    odd.append((-mi, None))
    half = count // 2
    from_even = real_sum(even, half, sorted({l // 2 for l in wanted if l % 2 == 0}))
    from_odd = real_sum(odd, half, sorted({l // 2 for l in wanted if l % 2 == 1}))
    return {l: (from_odd if l % 2 else from_even)[l // 2] for l in wanted}


def halves(value):
    high = value.astype(jnp.bfloat16)
    return high, (value - high.astype(jnp.float32)).astype(jnp.bfloat16)


def dot3(value, table):
    high, low = halves(value)
    dot = functools.partial(jnp.dot, preferred_element_type=jnp.float32)
    return dot(high, table[0]) + (dot(low, table[0]) + dot(high, table[1]))


def spectra(x_ref, small, forward, base):
    values = [x_ref[pl.ds(base * RADIX + n1, CHUNK, stride=RADIX), :] for n1 in range(RADIX)]
    turned_re, turned_im = [], []
    for s, (re, im) in enumerate(real_dft(values)):
        c, n = small[s : s + 1, :], small[17 + s : 18 + s, :]
        if s == 0:
            turned_re.append(re)
            turned_im.append(jnp.zeros_like(re))
        elif im is None:
            turned_re.append(re * c)
            turned_im.append(-re * n)
        else:
            turned_re.append(re * c + im * n)
            turned_im.append(im * c - re * n)
    rows = jnp.concatenate(
        [jnp.concatenate(turned_re, axis=0), jnp.concatenate(turned_im, axis=0)], axis=1
    )
    final = dot3(rows, forward)
    re = [final[s * CHUNK : (s + 1) * CHUNK, :LANES] for s in range(17)]
    im = [final[s * CHUNK : (s + 1) * CHUNK, LANES:] for s in range(17)]
    first = lax.broadcasted_iota(jnp.int32, (CHUNK, LANES), 1) < LANES // 2
    re[0] = jnp.where(first, re[16], re[0])
    im[0] = jnp.where(first, im[16], im[0])
    return re[:16], im[:16]


def whitened(re, im, small):
    lane = lax.broadcasted_iota(jnp.int32, (CHUNK, LANES), 1)
    first = lane < LANES // 2
    k2 = lane % (LANES // 2)
    size = [jnp.sqrt(a * a + b * b) for a, b in zip(re, im)]
    running = [jnp.zeros_like(size[0])]
    for s in range(1, SLABS):
        running.append(running[-1] + size[s])
    total = running[15] + size[0]
    total = total + pltpu.roll(total, LANES // 2, 1)
    centre = (
        total
        + jnp.where(k2 >= 1, pltpu.roll(total, 1, 1), 0.0)
        + jnp.where(k2 <= 62, pltpu.roll(total, LANES - 1, 1), 0.0)
    )
    before = pltpu.roll(running[15] + size[0], LANES // 2, 1) + running[15]
    out = []
    for s in range(SLABS):
        if s == 0:
            prefix = jnp.where(first, running[15] + size[0], total)
            suffix = jnp.where(first, total - running[15], size[0])
        else:
            prefix = jnp.where(first, running[s], before - running[s - 1])
            suffix = jnp.where(first, total - running[s - 1], running[s] + size[0])
        window = (
            centre
            + jnp.where(k2 >= 2, pltpu.roll(suffix, 2, 1), 0.0)
            + jnp.where(k2 <= 61, pltpu.roll(prefix, LANES - 2, 1), 0.0)
        )
        counted = small[34 + s : 35 + s, :]
        scale = counted / (window + EPSILON * counted)
        out.append((re[s] * scale, im[s] * scale))
    return out


def kernel(
    rows,
    traces,
    pair_list,
    live_pairs,
    forward_hbm,
    inverse_hbm,
    small_hbm,
    out_ref,
    members,
    live,
    x_ref,
    forward,
    inverse,
    small,
    turn,
    ext,
    cross_out,
    cross_own,
    cross_in,
    load_sem,
    table_sem,
    send_sem,
    recv_sem,
    swap_sem,
):
    me = lax.axis_index("pair")
    core = lax.axis_index("tm")
    count = lax.axis_size("pair")
    chunks = rows // CHUNK
    loads = [
        pltpu.make_async_copy(
            traces.at[pl.ds(i * CHUNK * RADIX, CHUNK * RADIX)],
            x_ref.at[pl.ds(i * CHUNK * RADIX, CHUNK * RADIX)],
            load_sem.at[i],
        )
        for i in range(chunks)
    ]
    table_loads = [
        pltpu.make_async_copy(src, dst, table_sem.at[i])
        for i, (src, dst) in enumerate(
            [
                (small_hbm, small),
                (forward_hbm, forward),
                (inverse_hbm, inverse),
                (pair_list, members),
                (live_pairs, live),
            ]
        )
    ]
    loads[0].start()
    table_loads[0].start()
    table_loads[1].start()
    for copy in loads[1:]:
        copy.start()
    for copy in table_loads[2:]:
        copy.start()

    barrier = pltpu.get_barrier_semaphore()

    def greet(target):
        pl.semaphore_signal(barrier, inc=1, device_id=target, device_id_type=MESH)

    has_before, has_after = me > 0, me < count - 1
    pl.when(has_before)(lambda: greet((me - 1, core)))
    pl.when(has_after)(lambda: greet((me + 1, core)))
    greet((me, 1 - core))

    def send(way, i):
        step, place = ((-1, 2 * rows), (1, 0))[way]
        return pltpu.make_async_remote_copy(
            src_ref=ext.at[pl.ds(rows + i * CHUNK, CHUNK)],
            dst_ref=ext.at[pl.ds(place + i * CHUNK, CHUNK)],
            send_sem=send_sem.at[way, i],
            recv_sem=recv_sem.at[way, i],
            device_id=(me + step, core),
            device_id_type=MESH,
        )

    for i in range(chunks):
        loads[i].wait()
        if i == 0:
            table_loads[0].wait()
            table_loads[1].wait()
        re, im = spectra(x_ref, small, forward, i * CHUNK)
        for s, (a, b) in enumerate(whitened(re, im, small)):
            place = i * CHUNK * 32 + s // 8 * 16 + s % 8
            turn[pl.ds(place, CHUNK, stride=32), :] = a
            turn[pl.ds(place + 8, CHUNK, stride=32), :] = b
        own = pl.ds(rows + i * CHUNK, CHUNK)
        part = turn[pl.ds(i * CHUNK * 32, CHUNK * 32), :].reshape(CHUNK, 2, 16, LANES)
        ext[own] = part.astype(jnp.bfloat16)
        if i == 0:
            pl.semaphore_wait(barrier, 1 + has_before.astype(jnp.int32) + has_after.astype(jnp.int32))
        pl.when(has_before)(lambda: send(0, i).start())
        pl.when(has_after)(lambda: send(1, i).start())

    @pl.when(has_after)
    def _():
        for i in range(chunks):
            send(0, i).wait_recv()

    @pl.when(has_before)
    def _():
        for i in range(chunks):
            send(1, i).wait_recv()

    table_loads[3].wait()
    table_loads[4].wait()
    anchor = me * rows - rows
    kept = rows // 2

    def cross(into, slot, i):
        first = jnp.clip(members[0, slot] - anchor, 0, 3 * rows - 1)
        second = jnp.clip(members[1, slot] - anchor, 0, 3 * rows - 1)
        for g in range(2):
            a = ext[first, g].astype(jnp.float32)
            b = ext[second, g].astype(jnp.float32)
            ar, ai, br, bi = a[:8], a[8:], b[:8], b[8:]
            place = pl.ds(g * 8 * kept + i, 8, stride=kept)
            into[0, place, :] = ar * br + ai * bi
            into[1, place, :] = ai * br - ar * bi

    for i in range(kept):
        cross(cross_out, (1 - core) * kept + i, i)
    swap = pltpu.make_async_remote_copy(
        src_ref=cross_out,
        dst_ref=cross_in,
        send_sem=swap_sem.at[0],
        recv_sem=swap_sem.at[1],
        device_id=(me, 1 - core),
        device_id_type=MESH,
    )
    swap.start()
    for i in range(kept):
        cross(cross_own, core * kept + i, i)
    table_loads[2].wait()
    swap.wait()

    both = jnp.concatenate(
        [cross_own[0] + cross_in[0], cross_own[1] + cross_in[1]], axis=1
    )
    lane = lax.broadcasted_iota(jnp.int32, (kept, 2 * LANES), 1) % LANES
    zeroth = both[:kept]
    spread = jnp.concatenate(
        [
            jnp.where(lane < LANES // 2, 0.0, zeroth),
            both[kept:],
            jnp.where(lane < LANES // 2, zeroth, 0.0),
        ],
        axis=0,
    )
    lags = dot3(spread, inverse)
    for part in range(kept // 8):
        bins = []
        for s in range(17):
            place = slice(s * kept + part * 8, s * kept + part * 8 + 8)
            vr, vi = lags[place, :LANES], lags[place, LANES:]
            c, n = small[s : s + 1, :], small[17 + s : 18 + s, :]
            if s == 0:
                bins.append((vr, None))
            elif s == 16:
                bins.append((vr * c - vi * n, None))
            else:
                bins.append((vr * c - vi * n, vr * n + vi * c))
        blocks = real_sum(bins, RADIX, [l1 % RADIX for l1 in range(-8, 8)])
        slot = core * kept + part * 8 + lax.broadcasted_iota(jnp.int32, (8, LANES), 0)
        wanted = slot < live[0]
        for l1 in range(-8, 8):
            out_ref[part * 8 : part * 8 + 8, (l1 + 8) * LANES : (l1 + 9) * LANES] = jnp.where(
                wanted, blocks[l1 % RADIX], 0.0
            )

    @pl.when(has_before)
    def _():
        for i in range(chunks):
            send(0, i).wait_send()

    @pl.when(has_after)
    def _():
        for i in range(chunks):
            send(1, i).wait_send()


def shards(traces, pair_list, live_pairs):
    rows = traces.shape[0]
    kept = rows // 2
    chunks = rows // CHUNK
    forward, inverse, small = tables()
    in_hbm = pl.BlockSpec(memory_space=pltpu.HBM)
    f32, bf16 = jnp.float32, jnp.bfloat16
    return pl.pallas_call(
        functools.partial(kernel, rows),
        out_shape=jax.ShapeDtypeStruct((kept, NLAG), f32),
        in_specs=[in_hbm] * 6,
        out_specs=pl.BlockSpec(memory_space=pltpu.VMEM),
        scratch_shapes=[
            pltpu.SMEM((2, rows), jnp.int32),
            pltpu.SMEM((1,), jnp.int32),
            pltpu.VMEM((rows * RADIX, LANES), f32),
            pltpu.VMEM(forward.shape, bf16),
            pltpu.VMEM(inverse.shape, bf16),
            pltpu.VMEM(small.shape, f32),
            pltpu.VMEM((rows * 32, LANES), f32),
            pltpu.VMEM((3 * rows, 2, 16, LANES), bf16),
            pltpu.VMEM((2, SLABS * kept, LANES), f32),
            pltpu.VMEM((2, SLABS * kept, LANES), f32),
            pltpu.VMEM((2, SLABS * kept, LANES), f32),
            pltpu.SemaphoreType.DMA((chunks,)),
            pltpu.SemaphoreType.DMA((5,)),
            pltpu.SemaphoreType.DMA((2, chunks)),
            pltpu.SemaphoreType.DMA((2, chunks)),
            pltpu.SemaphoreType.DMA((2,)),
        ],
        compiler_params=pltpu.CompilerParams(
            collective_id=0, has_side_effects=True, vmem_limit_bytes=60 * 1024 * 1024
        ),
        name="correlate",
    )(
        traces.reshape(rows * RADIX, LANES),
        pair_list.T,
        live_pairs,
        jnp.asarray(forward),
        jnp.asarray(inverse),
        jnp.asarray(small),
    )


def solution(mesh):
    placed = (P("pair", "tm", None), P("pair", None), P("pair"))
    return jax.shard_map(
        shards, mesh=mesh, in_specs=placed, out_specs=P(("pair", "tm"), None), check_vma=False
    )
```

```python
import functools
import math

import jax
import jax.numpy as jnp
import numpy as np
from jax import lax
from jax.experimental import pallas as pl
from jax.experimental.pallas import tpu as pltpu
from jax.sharding import PartitionSpec as P

NT = 4096
FB = 2048
NLAG = 2048
HALF = 64
EPSILON = 1e-06

RADIX = 32
LANES = 128
SLABS = 16
CHUNK = 8
MESH = pl.DeviceIdType.MESH


def split(table):
    high = table.astype(jnp.bfloat16)
    low = (table - high.astype(np.float64)).astype(jnp.bfloat16)
    return np.stack([high, low])


def tables():
    n0 = np.arange(LANES)
    k2 = np.arange(LANES // 2)
    q = np.concatenate([k2, LANES - 1 - k2])
    sign = np.concatenate([np.ones(LANES // 2), -np.ones(LANES // 2)])
    angle = 2.0 * math.pi * (n0[:, None] * q[None, :] % LANES) / LANES
    cos, sin = np.cos(angle), np.sin(angle)
    forward = np.block([[cos, -sin * sign], [sin, cos * sign]])
    inverse = np.block([[cos.T, sin.T], [-sin.T * sign[:, None], cos.T * sign[:, None]]])
    inverse = inverse / 64.0
    s = np.arange(SLABS + 1)
    twist = 2.0 * math.pi * (s[:, None] * n0[None, :]) / NT
    k1 = np.stack([np.where(s[:16] == 0, 16, s[:16]), 32 - s[:16]], axis=1)
    index = (k1[:, :, None] - 1 + RADIX * k2[None, None, :]).reshape(SLABS, LANES)
    counted = np.minimum(index + HALF, FB - 1) - np.maximum(index - HALF, 0) + 1
    small = np.zeros((56, LANES))
    small[0:17] = np.cos(twist)
    small[17:34] = np.sin(twist)
    small[34:50] = counted
    return split(forward), split(inverse), small.astype(np.float32)


def scaled(value, factor):
    return value if factor == 1.0 else -value if factor == -1.0 else value * factor


def real_dft(values):
    count = len(values)
    if count == 2:
        return [(values[0] + values[1], None), (values[0] - values[1], None)]
    even, odd = real_dft(values[0::2]), real_dft(values[1::2])
    quarter = count // 4
    bins = [None] * (count // 2 + 1)
    bins[0] = (even[0][0] + odd[0][0], None)
    bins[count // 2] = (even[0][0] - odd[0][0], None)
    for k in range(1, quarter):
        c, s = math.cos(2.0 * math.pi * k / count), math.sin(2.0 * math.pi * k / count)
        (er, ei), (pr, pi) = even[k], odd[k]
        if 8 * k == count:
            tr, ti = (pr + pi) * c, (pi - pr) * c
        else:
            tr, ti = pr * c + pi * s, pi * c - pr * s
        bins[k] = (er + tr, ei + ti)
        bins[count // 2 - k] = (er - tr, ti - ei)
    er, pr = even[quarter][0], odd[quarter][0]
    bins[quarter] = (er, -pr)
    return bins


def real_sum(bins, count, wanted):
    if count == 2:
        (ar, _), (br, _) = bins
        return {l: ar + br if l == 0 else ar - br for l in wanted}
    quarter = count // 4
    even, odd = [], []
    for s in range(quarter):
        (ar, ai), (br, bi) = bins[s], bins[count // 2 - s]
        if s == 0:
            even.append((ar + br, None))
            odd.append((ar - br, None))
            continue
        even.append((ar + br, ai - bi))
        dr, di = ar - br, ai + bi
        c, n = math.cos(2.0 * math.pi * s / count), math.sin(2.0 * math.pi * s / count)
        if 8 * s == count:
            odd.append(((dr - di) * c, (dr + di) * c))
        else:
            odd.append((dr * c - di * n, dr * n + di * c))
    mr, mi = bins[quarter]
    even.append((mr, None))
    odd.append((-mi, None))
    half = count // 2
    from_even = real_sum(even, half, sorted({l // 2 for l in wanted if l % 2 == 0}))
    from_odd = real_sum(odd, half, sorted({l // 2 for l in wanted if l % 2 == 1}))
    return {l: (from_odd if l % 2 else from_even)[l // 2] for l in wanted}


def halves(value):
    high = value.astype(jnp.bfloat16)
    return high, (value - high.astype(jnp.float32)).astype(jnp.bfloat16)


def dot3(value, table):
    high, low = halves(value)
    dot = functools.partial(jnp.dot, preferred_element_type=jnp.float32)
    return dot(high, table[0]) + (dot(low, table[0]) + dot(high, table[1]))


def spectra(x_ref, small, forward, base):
    first = pl.multiple_of(base * RADIX, CHUNK * RADIX)
    values = [x_ref[pl.ds(first + n1, CHUNK, stride=RADIX), :] for n1 in range(RADIX)]
    turned_re, turned_im = [], []
    for s, (re, im) in enumerate(real_dft(values)):
        c, n = small[s : s + 1, :], small[17 + s : 18 + s, :]
        if s == 0:
            turned_re.append(re)
            turned_im.append(jnp.zeros_like(re))
        elif im is None:
            turned_re.append(re * c)
            turned_im.append(-re * n)
        else:
            turned_re.append(re * c + im * n)
            turned_im.append(im * c - re * n)
    rows = jnp.concatenate(
        [jnp.concatenate(turned_re, axis=0), jnp.concatenate(turned_im, axis=0)], axis=1
    )
    final = dot3(rows, forward)
    re = [final[s * CHUNK : (s + 1) * CHUNK, :LANES] for s in range(17)]
    im = [final[s * CHUNK : (s + 1) * CHUNK, LANES:] for s in range(17)]
    first = lax.broadcasted_iota(jnp.int32, (CHUNK, LANES), 1) < LANES // 2
    re[0] = jnp.where(first, re[16], re[0])
    im[0] = jnp.where(first, im[16], im[0])
    return re[:16], im[:16]


def whitened(re, im, small):
    lane = lax.broadcasted_iota(jnp.int32, (CHUNK, LANES), 1)
    first = lane < LANES // 2
    k2 = lane % (LANES // 2)
    size = [jnp.sqrt(a * a + b * b) for a, b in zip(re, im)]
    running = [jnp.zeros_like(size[0])]
    for s in range(1, SLABS):
        running.append(running[-1] + size[s])
    total = running[15] + size[0]
    total = total + pltpu.roll(total, LANES // 2, 1)
    centre = (
        total
        + jnp.where(k2 >= 1, pltpu.roll(total, 1, 1), 0.0)
        + jnp.where(k2 <= 62, pltpu.roll(total, LANES - 1, 1), 0.0)
    )
    before = pltpu.roll(running[15] + size[0], LANES // 2, 1) + running[15]
    out = []
    for s in range(SLABS):
        if s == 0:
            prefix = jnp.where(first, running[15] + size[0], total)
            suffix = jnp.where(first, total - running[15], size[0])
        else:
            prefix = jnp.where(first, running[s], before - running[s - 1])
            suffix = jnp.where(first, total - running[s - 1], running[s] + size[0])
        window = (
            centre
            + jnp.where(k2 >= 2, pltpu.roll(suffix, 2, 1), 0.0)
            + jnp.where(k2 <= 61, pltpu.roll(prefix, LANES - 2, 1), 0.0)
        )
        counted = small[34 + s : 35 + s, :]
        scale = counted / (window + EPSILON * counted)
        out.append((re[s] * scale, im[s] * scale))
    return out


def kernel(
    rows,
    traces,
    pair_list,
    live_pairs,
    forward_hbm,
    inverse_hbm,
    small_hbm,
    out_ref,
    members,
    live,
    x_ref,
    forward,
    inverse,
    small,
    turn,
    ext_0,
    ext_1,
    cross_out,
    cross_own,
    cross_in,
    load_sem,
    table_sem,
    send_sem,
    recv_sem,
    swap_sem,
):
    me = lax.axis_index("pair")
    core = lax.axis_index("tm")
    count = lax.axis_size("pair")
    chunks = rows // CHUNK
    kept = rows // 2
    ext = (ext_0, ext_1)

    def load(i):
        size = CHUNK * RADIX
        place = pl.ds(pl.multiple_of(i * size, size), size)
        return pltpu.make_async_copy(traces.at[place], x_ref.at[place], load_sem.at[i])

    table_loads = [
        pltpu.make_async_copy(src, dst, table_sem.at[i])
        for i, (src, dst) in enumerate(
            [
                (small_hbm, small),
                (forward_hbm, forward),
                (inverse_hbm, inverse),
                (pair_list, members),
                (live_pairs, live),
            ]
        )
    ]
    load(0).start()
    table_loads[0].start()
    table_loads[1].start()
    for i in range(1, chunks):
        load(i).start()
    for copy in table_loads[2:]:
        copy.start()

    first = (me == 0).astype(jnp.int32)
    last = (me == count - 1).astype(jnp.int32)
    other = 1 - core
    ways = (
        ((me - 1 + first, core + first * (other - core)), 2 * rows * (1 - first), first),
        ((me + 1 - last, core + last * (other - core)), 2 * rows * last, 1 - last),
    )
    barrier = pltpu.get_barrier_semaphore()
    for target in (ways[0][0], ways[1][0], (me, other)):
        pl.semaphore_signal(barrier, inc=1, device_id=target, device_id_type=MESH)

    def send(way, part):
        target, place, semaphore = ways[way]
        whole = isinstance(part, int) and part == chunks
        half, start, size = (1, 0, rows) if whole else (0, part * CHUNK, CHUNK)
        return pltpu.make_async_remote_copy(
            src_ref=ext[half].at[pl.ds(rows + start, size)],
            dst_ref=ext[half].at[pl.ds(place + start, size)],
            send_sem=send_sem.at[way, part],
            recv_sem=recv_sem.at[semaphore, part],
            device_id=target,
            device_id_type=MESH,
        )

    def arrival(side, part):
        half, start, size = (0, part * CHUNK, CHUNK) if part < chunks else (1, 0, rows)
        place = ext[half].at[pl.ds((1 - side) * 2 * rows + start, size)]
        return pltpu.make_async_remote_copy(
            src_ref=place,
            dst_ref=place,
            send_sem=send_sem.at[0, part],
            recv_sem=recv_sem.at[side, part],
            device_id=(me, other),
            device_id_type=MESH,
        )

    table_loads[0].wait()
    table_loads[1].wait()

    def transform(i, carry):
        start = pl.multiple_of(i * CHUNK, CHUNK)
        load(i).wait()
        re, im = spectra(x_ref, small, forward, start)
        for s, (a, b) in enumerate(whitened(re, im, small)):
            place = s // 8 * 16 + s % 8
            turn[pl.ds(place, CHUNK, stride=32), :] = a
            turn[pl.ds(place + 8, CHUNK, stride=32), :] = b
        part = turn[...].reshape(CHUNK, 2, 16, LANES)
        for half in range(2):
            ext[half][pl.ds(rows + start, CHUNK)] = part[:, half].astype(jnp.bfloat16)

        @pl.when(i == 0)
        def _():
            pl.semaphore_wait(barrier, 3)

        for way in range(2):
            send(way, i).start()
        return carry

    lax.fori_loop(0, chunks, transform, 0)
    for way in range(2):
        send(way, chunks).start()

    table_loads[3].wait()
    table_loads[4].wait()
    anchor = me * rows - rows

    def cross(half, into, slot, i):
        one = jnp.clip(members[0, slot] - anchor, 0, 3 * rows - 1)
        two = jnp.clip(members[1, slot] - anchor, 0, 3 * rows - 1)
        a = ext[half][one].astype(jnp.float32)
        b = ext[half][two].astype(jnp.float32)
        ar, ai, br, bi = a[:8], a[8:], b[:8], b[8:]
        place = pl.ds(i, 8, stride=kept)
        into[half, 0, place, :] = ar * br + ai * bi
        into[half, 1, place, :] = ai * br - ar * bi

    def swap(half):
        return pltpu.make_async_remote_copy(
            src_ref=cross_out.at[half],
            dst_ref=cross_in.at[half],
            send_sem=swap_sem.at[0, half],
            recv_sem=swap_sem.at[1, half],
            device_id=(me, other),
            device_id_type=MESH,
        )

    for half in range(2):
        for side in range(2):
            for part in range(chunks) if half == 0 else [chunks]:
                arrival(side, part).wait_recv()
        for i in range(kept):
            cross(half, cross_out, other * kept + i, i)
        swap(half).start()
        for i in range(kept):
            cross(half, cross_own, core * kept + i, i)
    table_loads[2].wait()

    lane = lax.broadcasted_iota(jnp.int32, (kept, 2 * LANES), 1) % LANES
    parts = []
    for half in range(2):
        swap(half).wait()
        both = jnp.concatenate(
            [cross_own[half, i] + cross_in[half, i] for i in range(2)], axis=1
        )
        if half == 0:
            zeroth = both[:kept]
            parts += [jnp.where(lane < LANES // 2, 0.0, zeroth), both[kept:]]
        else:
            parts += [both, jnp.where(lane < LANES // 2, zeroth, 0.0)]
    lags = dot3(jnp.concatenate(parts, axis=0), inverse)
    for part in range(kept // 8):
        bins = []
        for s in range(17):
            place = slice(s * kept + part * 8, s * kept + part * 8 + 8)
            vr, vi = lags[place, :LANES], lags[place, LANES:]
            c, n = small[s : s + 1, :], small[17 + s : 18 + s, :]
            if s == 0:
                bins.append((vr, None))
            elif s == 16:
                bins.append((vr * c - vi * n, None))
            else:
                bins.append((vr * c - vi * n, vr * n + vi * c))
        blocks = real_sum(bins, RADIX, [l1 % RADIX for l1 in range(-8, 8)])
        slot = core * kept + part * 8 + lax.broadcasted_iota(jnp.int32, (8, LANES), 0)
        wanted = slot < live[0]
        for l1 in range(-8, 8):
            out_ref[part * 8 : part * 8 + 8, (l1 + 8) * LANES : (l1 + 9) * LANES] = jnp.where(
                wanted, blocks[l1 % RADIX], 0.0
            )
    for way in range(2):
        for part in range(chunks + 1):
            send(way, part).wait_send()


def shards(traces, pair_list, live_pairs):
    rows = traces.shape[0]
    kept = rows // 2
    chunks = rows // CHUNK
    forward, inverse, small = tables()
    in_place = functools.partial(pltpu.with_memory_space_constraint, memory_space=pltpu.HBM)
    in_hbm = pl.BlockSpec(memory_space=pltpu.HBM)
    f32, bf16 = jnp.float32, jnp.bfloat16
    return pl.pallas_call(
        functools.partial(kernel, rows),
        out_shape=jax.ShapeDtypeStruct((kept, NLAG), f32),
        in_specs=[in_hbm] * 6,
        out_specs=pl.BlockSpec(memory_space=pltpu.VMEM),
        scratch_shapes=[
            pltpu.SMEM((2, rows), jnp.int32),
            pltpu.SMEM((1,), jnp.int32),
            pltpu.VMEM((rows * RADIX, LANES), f32),
            pltpu.VMEM(forward.shape, bf16),
            pltpu.VMEM(inverse.shape, bf16),
            pltpu.VMEM(small.shape, f32),
            pltpu.VMEM((CHUNK * 32, LANES), f32),
            pltpu.VMEM((3 * rows, 16, LANES), bf16),
            pltpu.VMEM((3 * rows, 16, LANES), bf16),
            pltpu.VMEM((2, 2, 8 * kept, LANES), f32),
            pltpu.VMEM((2, 2, 8 * kept, LANES), f32),
            pltpu.VMEM((2, 2, 8 * kept, LANES), f32),
            pltpu.SemaphoreType.DMA((chunks,)),
            pltpu.SemaphoreType.DMA((5,)),
            pltpu.SemaphoreType.DMA((2, chunks + 1)),
            pltpu.SemaphoreType.DMA((2, chunks + 1)),
            pltpu.SemaphoreType.DMA((2, 2)),
        ],
        compiler_params=pltpu.CompilerParams(
            collective_id=0, has_side_effects=True, vmem_limit_bytes=32 * 1024 * 1024
        ),
        name="correlate",
    )(
        in_place(traces.reshape(rows * RADIX, LANES)),
        in_place(pair_list.T),
        live_pairs,
        in_place(jnp.asarray(forward)),
        in_place(jnp.asarray(inverse)),
        in_place(jnp.asarray(small)),
    )


def solution(mesh):
    placed = (P("pair", "tm", None), P("pair", None), P("pair"))
    return jax.shard_map(
        shards, mesh=mesh, in_specs=placed, out_specs=P(("pair", "tm"), None), check_vma=False
    )
```

```python
import functools
import math

import jax
import jax.numpy as jnp
import numpy as np
from jax import lax
from jax.experimental import pallas as pl
from jax.experimental.pallas import tpu as pltpu
from jax.sharding import PartitionSpec as P

NT = 4096
FB = 2048
NLAG = 2048
HALF = 64
EPSILON = 1e-06

RADIX = 32
LANES = 128
SLABS = 16
CHUNK = 8
MESH = pl.DeviceIdType.MESH


def split(table):
    high = table.astype(jnp.bfloat16)
    low = (table - high.astype(np.float64)).astype(jnp.bfloat16)
    return np.stack([high, low])


def tables():
    n0 = np.arange(LANES)
    k2 = np.arange(LANES // 2)
    q = np.concatenate([k2, LANES - 1 - k2])
    sign = np.concatenate([np.ones(LANES // 2), -np.ones(LANES // 2)])
    angle = 2.0 * math.pi * (n0[:, None] * q[None, :] % LANES) / LANES
    cos, sin = np.cos(angle), np.sin(angle)
    forward = np.block([[cos, -sin * sign], [sin, cos * sign]])
    inverse = np.block([[cos.T, sin.T], [-sin.T * sign[:, None], cos.T * sign[:, None]]])
    inverse = inverse / 64.0
    s = np.arange(SLABS + 1)
    twist = 2.0 * math.pi * (s[:, None] * n0[None, :]) / NT
    k1 = np.stack([np.where(s[:16] == 0, 16, s[:16]), 32 - s[:16]], axis=1)
    index = (k1[:, :, None] - 1 + RADIX * k2[None, None, :]).reshape(SLABS, LANES)
    counted = np.minimum(index + HALF, FB - 1) - np.maximum(index - HALF, 0) + 1
    small = np.zeros((56, LANES))
    small[0:17] = np.cos(twist)
    small[17:34] = np.sin(twist)
    small[34:50] = counted
    return split(forward), split(inverse), small.astype(np.float32)


def scaled(value, factor):
    return value if factor == 1.0 else -value if factor == -1.0 else value * factor


def real_dft(values):
    count = len(values)
    if count == 2:
        return [(values[0] + values[1], None), (values[0] - values[1], None)]
    even, odd = real_dft(values[0::2]), real_dft(values[1::2])
    quarter = count // 4
    bins = [None] * (count // 2 + 1)
    bins[0] = (even[0][0] + odd[0][0], None)
    bins[count // 2] = (even[0][0] - odd[0][0], None)
    for k in range(1, quarter):
        c, s = math.cos(2.0 * math.pi * k / count), math.sin(2.0 * math.pi * k / count)
        (er, ei), (pr, pi) = even[k], odd[k]
        if 8 * k == count:
            tr, ti = (pr + pi) * c, (pi - pr) * c
        else:
            tr, ti = pr * c + pi * s, pi * c - pr * s
        bins[k] = (er + tr, ei + ti)
        bins[count // 2 - k] = (er - tr, ti - ei)
    er, pr = even[quarter][0], odd[quarter][0]
    bins[quarter] = (er, -pr)
    return bins


def real_sum(bins, count, wanted):
    if count == 2:
        (ar, _), (br, _) = bins
        return {l: ar + br if l == 0 else ar - br for l in wanted}
    quarter = count // 4
    even, odd = [], []
    for s in range(quarter):
        (ar, ai), (br, bi) = bins[s], bins[count // 2 - s]
        if s == 0:
            even.append((ar + br, None))
            odd.append((ar - br, None))
            continue
        even.append((ar + br, ai - bi))
        dr, di = ar - br, ai + bi
        c, n = math.cos(2.0 * math.pi * s / count), math.sin(2.0 * math.pi * s / count)
        if 8 * s == count:
            odd.append(((dr - di) * c, (dr + di) * c))
        else:
            odd.append((dr * c - di * n, dr * n + di * c))
    mr, mi = bins[quarter]
    even.append((mr, None))
    odd.append((-mi, None))
    half = count // 2
    from_even = real_sum(even, half, sorted({l // 2 for l in wanted if l % 2 == 0}))
    from_odd = real_sum(odd, half, sorted({l // 2 for l in wanted if l % 2 == 1}))
    return {l: (from_odd if l % 2 else from_even)[l // 2] for l in wanted}


def halves(value):
    high = value.astype(jnp.bfloat16)
    return high, (value - high.astype(jnp.float32)).astype(jnp.bfloat16)


def dot3(value, table):
    high, low = halves(value)
    dot = functools.partial(jnp.dot, preferred_element_type=jnp.float32)
    return dot(high, table[0]) + (dot(low, table[0]) + dot(high, table[1]))


def spectra(x_ref, small, forward, base):
    first = pl.multiple_of(base * RADIX, CHUNK * RADIX)
    values = [x_ref[pl.ds(first + n1, CHUNK, stride=RADIX), :] for n1 in range(RADIX)]
    turned_re, turned_im = [], []
    for s, (re, im) in enumerate(real_dft(values)):
        c, n = small[s : s + 1, :], small[17 + s : 18 + s, :]
        if s == 0:
            turned_re.append(re)
            turned_im.append(jnp.zeros_like(re))
        elif im is None:
            turned_re.append(re * c)
            turned_im.append(-re * n)
        else:
            turned_re.append(re * c + im * n)
            turned_im.append(im * c - re * n)
    rows = jnp.concatenate(
        [jnp.concatenate(turned_re, axis=0), jnp.concatenate(turned_im, axis=0)], axis=1
    )
    final = dot3(rows, forward)
    re = [final[s * CHUNK : (s + 1) * CHUNK, :LANES] for s in range(17)]
    im = [final[s * CHUNK : (s + 1) * CHUNK, LANES:] for s in range(17)]
    first = lax.broadcasted_iota(jnp.int32, (CHUNK, LANES), 1) < LANES // 2
    re[0] = jnp.where(first, re[16], re[0])
    im[0] = jnp.where(first, im[16], im[0])
    return re[:16], im[:16]


def whitened(re, im, small):
    lane = lax.broadcasted_iota(jnp.int32, (CHUNK, LANES), 1)
    first = lane < LANES // 2
    k2 = lane % (LANES // 2)
    size = [jnp.sqrt(a * a + b * b) for a, b in zip(re, im)]
    running = [jnp.zeros_like(size[0])]
    for s in range(1, SLABS):
        running.append(running[-1] + size[s])
    total = running[15] + size[0]
    total = total + pltpu.roll(total, LANES // 2, 1)
    centre = (
        total
        + jnp.where(k2 >= 1, pltpu.roll(total, 1, 1), 0.0)
        + jnp.where(k2 <= 62, pltpu.roll(total, LANES - 1, 1), 0.0)
    )
    before = pltpu.roll(running[15] + size[0], LANES // 2, 1) + running[15]
    out = []
    for s in range(SLABS):
        if s == 0:
            prefix = jnp.where(first, running[15] + size[0], total)
            suffix = jnp.where(first, total - running[15], size[0])
        else:
            prefix = jnp.where(first, running[s], before - running[s - 1])
            suffix = jnp.where(first, total - running[s - 1], running[s] + size[0])
        window = (
            centre
            + jnp.where(k2 >= 2, pltpu.roll(suffix, 2, 1), 0.0)
            + jnp.where(k2 <= 61, pltpu.roll(prefix, LANES - 2, 1), 0.0)
        )
        counted = small[34 + s : 35 + s, :]
        scale = counted / (window + EPSILON * counted)
        out.append((re[s] * scale, im[s] * scale))
    return out


def kernel(
    rows,
    traces,
    pair_list,
    live_pairs,
    forward_hbm,
    inverse_hbm,
    small_hbm,
    out_ref,
    members,
    live,
    x_ref,
    forward,
    inverse,
    small,
    turn,
    ext_0,
    ext_1,
    cross_out,
    cross_own,
    cross_in,
    load_sem,
    table_sem,
    send_sem,
    recv_sem,
    swap_sem,
):
    me = lax.axis_index("pair")
    core = lax.axis_index("tm")
    count = lax.axis_size("pair")
    chunks = rows // CHUNK
    kept = rows // 2
    ext = (ext_0, ext_1)

    def load(i):
        place = (pl.ds(0, CHUNK * RADIX), pl.ds(CHUNK * RADIX, (rows - CHUNK) * RADIX))[i]
        return pltpu.make_async_copy(traces.at[place], x_ref.at[place], load_sem.at[i])

    table_loads = [
        pltpu.make_async_copy(src, dst, table_sem.at[i])
        for i, (src, dst) in enumerate(
            [
                (small_hbm, small),
                (forward_hbm, forward),
                (inverse_hbm, inverse),
                (pair_list, members),
                (live_pairs, live),
            ]
        )
    ]
    load(0).start()
    table_loads[0].start()
    table_loads[1].start()
    load(1).start()
    for copy in table_loads[2:]:
        copy.start()

    first = (me == 0).astype(jnp.int32)
    last = (me == count - 1).astype(jnp.int32)
    other = 1 - core
    ways = (
        ((me - 1 + first, core + first * (other - core)), 2 * rows * (1 - first), first),
        ((me + 1 - last, core + last * (other - core)), 2 * rows * last, 1 - last),
    )
    barrier = pltpu.get_barrier_semaphore()
    for target in (ways[0][0], ways[1][0], (me, other)):
        pl.semaphore_signal(barrier, inc=1, device_id=target, device_id_type=MESH)

    def send(way, half, start, size):
        target, place, side = ways[way]
        return pltpu.make_async_remote_copy(
            src_ref=ext[half].at[pl.ds(rows + start, size)],
            dst_ref=ext[half].at[pl.ds(place + start, size)],
            send_sem=send_sem.at[way, half],
            recv_sem=recv_sem.at[side, half],
            device_id=target,
            device_id_type=MESH,
        )

    def arrival(side, half):
        place = ext[half].at[pl.ds((1 - side) * 2 * rows, rows)]
        return pltpu.make_async_remote_copy(
            src_ref=place,
            dst_ref=place,
            send_sem=send_sem.at[0, half],
            recv_sem=recv_sem.at[side, half],
            device_id=(me, other),
            device_id_type=MESH,
        )

    load(0).wait()
    table_loads[0].wait()
    table_loads[1].wait()

    def transform(i, carry):
        start = pl.multiple_of(i * CHUNK, CHUNK)
        pl.when(i == 1)(load(1).wait)
        re, im = spectra(x_ref, small, forward, start)
        for s, (a, b) in enumerate(whitened(re, im, small)):
            place = s // 8 * 16 + s % 8
            turn[pl.ds(place, CHUNK, stride=32), :] = a
            turn[pl.ds(place + 8, CHUNK, stride=32), :] = b
        part = turn[...].reshape(CHUNK, 2, 16, LANES)
        for half in range(2):
            ext[half][pl.ds(rows + start, CHUNK)] = part[:, half].astype(jnp.bfloat16)

        @pl.when(i == 0)
        def _():
            pl.semaphore_wait(barrier, 3)

        for way in range(2):
            send(way, 0, start, CHUNK).start()

        @pl.when(i > 0)
        def _():
            for way in range(2):
                send(way, 1, start - CHUNK, CHUNK).start()

        return carry

    lax.fori_loop(0, chunks, transform, 0)
    for way in range(2):
        send(way, 1, rows - CHUNK, CHUNK).start()

    table_loads[3].wait()
    table_loads[4].wait()
    anchor = me * rows - rows

    def cross(half, into, slot, i):
        one = jnp.clip(members[0, slot] - anchor, 0, 3 * rows - 1)
        two = jnp.clip(members[1, slot] - anchor, 0, 3 * rows - 1)
        a = ext[half][one].astype(jnp.float32)
        b = ext[half][two].astype(jnp.float32)
        ar, ai, br, bi = a[:8], a[8:], b[:8], b[8:]
        place = pl.ds(i, 8, stride=kept)
        into[half, 0, place, :] = ar * br + ai * bi
        into[half, 1, place, :] = ai * br - ar * bi

    def swap(half):
        return pltpu.make_async_remote_copy(
            src_ref=cross_out.at[half],
            dst_ref=cross_in.at[half],
            send_sem=swap_sem.at[0, half],
            recv_sem=swap_sem.at[1, half],
            device_id=(me, other),
            device_id_type=MESH,
        )

    for half in range(2):
        for side in range(2):
            arrival(side, half).wait_recv()
        for i in range(kept):
            cross(half, cross_out, other * kept + i, i)
        swap(half).start()
        for i in range(kept):
            cross(half, cross_own, core * kept + i, i)
    table_loads[2].wait()

    lane = lax.broadcasted_iota(jnp.int32, (kept, 2 * LANES), 1) % LANES
    lags = []
    for half in range(2):
        swap(half).wait()
        both = jnp.concatenate(
            [cross_own[half, i] + cross_in[half, i] for i in range(2)], axis=1
        )
        if half == 0:
            zeroth = both[:kept]
            parts = [
                jnp.where(lane < LANES // 2, 0.0, zeroth),
                both[kept:],
                jnp.where(lane < LANES // 2, zeroth, 0.0),
            ]
            both = jnp.concatenate(parts, axis=0)
        lags.append(dot3(both, inverse))
    lags = jnp.concatenate([lags[0][: 8 * kept], lags[1], lags[0][8 * kept :]], axis=0)
    for part in range(kept // 8):
        bins = []
        for s in range(17):
            place = slice(s * kept + part * 8, s * kept + part * 8 + 8)
            vr, vi = lags[place, :LANES], lags[place, LANES:]
            c, n = small[s : s + 1, :], small[17 + s : 18 + s, :]
            if s == 0:
                bins.append((vr, None))
            elif s == 16:
                bins.append((vr * c - vi * n, None))
            else:
                bins.append((vr * c - vi * n, vr * n + vi * c))
        blocks = real_sum(bins, RADIX, [l1 % RADIX for l1 in range(-8, 8)])
        slot = core * kept + part * 8 + lax.broadcasted_iota(jnp.int32, (8, LANES), 0)
        wanted = slot < live[0]
        for l1 in range(-8, 8):
            out_ref[part * 8 : part * 8 + 8, (l1 + 8) * LANES : (l1 + 9) * LANES] = jnp.where(
                wanted, blocks[l1 % RADIX], 0.0
            )
    for way in range(2):
        for half in range(2):
            send(way, half, 0, rows).wait_send()


def shards(traces, pair_list, live_pairs):
    rows = traces.shape[0]
    kept = rows // 2
    chunks = rows // CHUNK
    forward, inverse, small = tables()
    in_place = functools.partial(pltpu.with_memory_space_constraint, memory_space=pltpu.HBM)
    in_hbm = pl.BlockSpec(memory_space=pltpu.HBM)
    f32, bf16 = jnp.float32, jnp.bfloat16
    return pl.pallas_call(
        functools.partial(kernel, rows),
        out_shape=jax.ShapeDtypeStruct((kept, NLAG), f32),
        in_specs=[in_hbm] * 6,
        out_specs=pl.BlockSpec(memory_space=pltpu.VMEM),
        scratch_shapes=[
            pltpu.SMEM((2, rows), jnp.int32),
            pltpu.SMEM((1,), jnp.int32),
            pltpu.VMEM((rows * RADIX, LANES), f32),
            pltpu.VMEM(forward.shape, bf16),
            pltpu.VMEM(inverse.shape, bf16),
            pltpu.VMEM(small.shape, f32),
            pltpu.VMEM((CHUNK * 32, LANES), f32),
            pltpu.VMEM((3 * rows, 16, LANES), bf16),
            pltpu.VMEM((3 * rows, 16, LANES), bf16),
            pltpu.VMEM((2, 2, 8 * kept, LANES), f32),
            pltpu.VMEM((2, 2, 8 * kept, LANES), f32),
            pltpu.VMEM((2, 2, 8 * kept, LANES), f32),
            pltpu.SemaphoreType.DMA((2,)),
            pltpu.SemaphoreType.DMA((5,)),
            pltpu.SemaphoreType.DMA((2, 2)),
            pltpu.SemaphoreType.DMA((2, 2)),
            pltpu.SemaphoreType.DMA((2, 2)),
        ],
        compiler_params=pltpu.CompilerParams(
            collective_id=0, has_side_effects=True, vmem_limit_bytes=32 * 1024 * 1024
        ),
        name="correlate",
    )(
        in_place(traces.reshape(rows * RADIX, LANES)),
        in_place(pair_list.T),
        live_pairs,
        in_place(jnp.asarray(forward)),
        in_place(jnp.asarray(inverse)),
        in_place(jnp.asarray(small)),
    )


def solution(mesh):
    placed = (P("pair", "tm", None), P("pair", None), P("pair"))
    return jax.shard_map(
        shards, mesh=mesh, in_specs=placed, out_specs=P(("pair", "tm"), None), check_vma=False
    )
```

```python
import functools
import math

import jax
import jax.numpy as jnp
import numpy as np
from jax import lax
from jax.experimental import pallas as pl
from jax.experimental.pallas import tpu as pltpu
from jax.sharding import PartitionSpec as P

NT = 4096
FB = 2048
NLAG = 2048
HALF = 64
EPSILON = 1e-06

RADIX = 32
LANES = 128
SLABS = 16
CHUNK = 8
PITCH = 40
MESH = pl.DeviceIdType.MESH


def split(table):
    high = table.astype(jnp.bfloat16)
    low = (table - high.astype(np.float64)).astype(jnp.bfloat16)
    return np.stack([high, low])


def tables():
    n0 = np.arange(LANES)
    k2 = np.arange(LANES // 2)
    q = np.concatenate([k2, LANES - 1 - k2])
    sign = np.concatenate([np.ones(LANES // 2), -np.ones(LANES // 2)])
    angle = 2.0 * math.pi * (n0[:, None] * q[None, :] % LANES) / LANES
    cos, sin = np.cos(angle), np.sin(angle)
    forward = np.block([[cos, -sin * sign], [sin, cos * sign]])
    inverse = np.block([[cos.T, sin.T], [-sin.T * sign[:, None], cos.T * sign[:, None]]])
    inverse = inverse / 64.0
    s = np.arange(SLABS + 1)
    twist = 2.0 * math.pi * (s[:, None] * n0[None, :]) / NT
    k1 = np.stack([np.where(s[:16] == 0, 16, s[:16]), 32 - s[:16]], axis=1)
    index = (k1[:, :, None] - 1 + RADIX * k2[None, None, :]).reshape(SLABS, LANES)
    counted = np.minimum(index + HALF, FB - 1) - np.maximum(index - HALF, 0) + 1
    small = np.zeros((56, LANES))
    small[0:17] = np.cos(twist)
    small[17:34] = np.sin(twist)
    small[34:50] = counted
    return split(forward), split(inverse), small.astype(np.float32)


def scaled(value, factor):
    return value if factor == 1.0 else -value if factor == -1.0 else value * factor


def real_dft(values):
    count = len(values)
    if count == 2:
        return [(values[0] + values[1], None), (values[0] - values[1], None)]
    even, odd = real_dft(values[0::2]), real_dft(values[1::2])
    quarter = count // 4
    bins = [None] * (count // 2 + 1)
    bins[0] = (even[0][0] + odd[0][0], None)
    bins[count // 2] = (even[0][0] - odd[0][0], None)
    for k in range(1, quarter):
        c, s = math.cos(2.0 * math.pi * k / count), math.sin(2.0 * math.pi * k / count)
        (er, ei), (pr, pi) = even[k], odd[k]
        if 8 * k == count:
            tr, ti = (pr + pi) * c, (pi - pr) * c
        else:
            tr, ti = pr * c + pi * s, pi * c - pr * s
        bins[k] = (er + tr, ei + ti)
        bins[count // 2 - k] = (er - tr, ti - ei)
    er, pr = even[quarter][0], odd[quarter][0]
    bins[quarter] = (er, -pr)
    return bins


def real_sum(bins, count, wanted):
    if count == 2:
        (ar, _), (br, _) = bins
        return {l: ar + br if l == 0 else ar - br for l in wanted}
    quarter = count // 4
    even, odd = [], []
    for s in range(quarter):
        (ar, ai), (br, bi) = bins[s], bins[count // 2 - s]
        if s == 0:
            even.append((ar + br, None))
            odd.append((ar - br, None))
            continue
        even.append((ar + br, ai - bi))
        dr, di = ar - br, ai + bi
        c, n = math.cos(2.0 * math.pi * s / count), math.sin(2.0 * math.pi * s / count)
        if 8 * s == count:
            odd.append(((dr - di) * c, (dr + di) * c))
        else:
            odd.append((dr * c - di * n, dr * n + di * c))
    mr, mi = bins[quarter]
    even.append((mr, None))
    odd.append((-mi, None))
    half = count // 2
    from_even = real_sum(even, half, sorted({l // 2 for l in wanted if l % 2 == 0}))
    from_odd = real_sum(odd, half, sorted({l // 2 for l in wanted if l % 2 == 1}))
    return {l: (from_odd if l % 2 else from_even)[l // 2] for l in wanted}


def halves(value):
    high = value.astype(jnp.bfloat16)
    return high, (value - high.astype(jnp.float32)).astype(jnp.bfloat16)


def dot3(value, table):
    high, low = halves(value)
    dot = functools.partial(jnp.dot, preferred_element_type=jnp.float32)
    return dot(high, table[0]) + (dot(low, table[0]) + dot(high, table[1]))


def spectra(x_ref, small, forward, base):
    first = pl.multiple_of(base * RADIX, CHUNK * RADIX)
    values = [x_ref[pl.ds(first + n1, CHUNK, stride=RADIX), :] for n1 in range(RADIX)]
    turned_re, turned_im = [], []
    for s, (re, im) in enumerate(real_dft(values)):
        c, n = small[s : s + 1, :], small[17 + s : 18 + s, :]
        if s == 0:
            turned_re.append(re)
            turned_im.append(jnp.zeros_like(re))
        elif im is None:
            turned_re.append(re * c)
            turned_im.append(-re * n)
        else:
            turned_re.append(re * c + im * n)
            turned_im.append(im * c - re * n)
    rows = jnp.concatenate(
        [jnp.concatenate(turned_re, axis=0), jnp.concatenate(turned_im, axis=0)], axis=1
    )
    final = dot3(rows, forward)
    re = [final[s * CHUNK : (s + 1) * CHUNK, :LANES] for s in range(17)]
    im = [final[s * CHUNK : (s + 1) * CHUNK, LANES:] for s in range(17)]
    first = lax.broadcasted_iota(jnp.int32, (CHUNK, LANES), 1) < LANES // 2
    re[0] = jnp.where(first, re[16], re[0])
    im[0] = jnp.where(first, im[16], im[0])
    return re[:16], im[:16]


def whitened(re, im, small):
    lane = lax.broadcasted_iota(jnp.int32, (CHUNK, LANES), 1)
    first = lane < LANES // 2
    k2 = lane % (LANES // 2)
    size = [jnp.sqrt(a * a + b * b) for a, b in zip(re, im)]
    running = [jnp.zeros_like(size[0])]
    for s in range(1, SLABS):
        running.append(running[-1] + size[s])
    total = running[15] + size[0]
    total = total + pltpu.roll(total, LANES // 2, 1)
    centre = (
        total
        + jnp.where(k2 >= 1, pltpu.roll(total, 1, 1), 0.0)
        + jnp.where(k2 <= 62, pltpu.roll(total, LANES - 1, 1), 0.0)
    )
    before = pltpu.roll(running[15] + size[0], LANES // 2, 1) + running[15]
    out = []
    for s in range(SLABS):
        if s == 0:
            prefix = jnp.where(first, running[15] + size[0], total)
            suffix = jnp.where(first, total - running[15], size[0])
        else:
            prefix = jnp.where(first, running[s], before - running[s - 1])
            suffix = jnp.where(first, total - running[s - 1], running[s] + size[0])
        window = (
            centre
            + jnp.where(k2 >= 2, pltpu.roll(suffix, 2, 1), 0.0)
            + jnp.where(k2 <= 61, pltpu.roll(prefix, LANES - 2, 1), 0.0)
        )
        counted = small[34 + s : 35 + s, :]
        scale = counted / (window + EPSILON * counted)
        out.append((re[s] * scale, im[s] * scale))
    return out


def kernel(
    rows,
    traces,
    pair_list,
    live_pairs,
    forward_hbm,
    inverse_hbm,
    small_hbm,
    out_ref,
    members,
    live,
    x_ref,
    forward,
    inverse,
    small,
    turn,
    ext_0,
    ext_1,
    cross_out,
    cross_own,
    cross_in,
    load_sem,
    table_sem,
    send_sem,
    recv_sem,
    swap_sem,
):
    me = lax.axis_index("pair")
    core = lax.axis_index("tm")
    count = lax.axis_size("pair")
    chunks = rows // CHUNK
    kept = rows // 2
    ext = (ext_0, ext_1)

    def load(i):
        place = (pl.ds(0, CHUNK * RADIX), pl.ds(CHUNK * RADIX, (rows - CHUNK) * RADIX))[i]
        return pltpu.make_async_copy(traces.at[place], x_ref.at[place], load_sem.at[i])

    table_loads = [
        pltpu.make_async_copy(src, dst, table_sem.at[i])
        for i, (src, dst) in enumerate(
            [
                (small_hbm, small),
                (forward_hbm, forward),
                (inverse_hbm, inverse),
                (pair_list, members),
                (live_pairs, live),
            ]
        )
    ]
    first = (me == 0).astype(jnp.int32)
    last = (me == count - 1).astype(jnp.int32)
    other = 1 - core
    ways = (
        ((me - 1 + first, core + first * (other - core)), 2 * rows * (1 - first), first),
        ((me + 1 - last, core + last * (other - core)), 2 * rows * last, 1 - last),
    )
    barrier = pltpu.get_barrier_semaphore()
    for target in (ways[0][0], ways[1][0], (me, other)):
        pl.semaphore_signal(barrier, inc=1, device_id=target, device_id_type=MESH)

    load(0).start()
    table_loads[0].start()
    table_loads[1].start()
    load(1).start()
    for copy in table_loads[2:]:
        copy.start()

    def send(way, half, start, size):
        target, place, side = ways[way]
        return pltpu.make_async_remote_copy(
            src_ref=ext[half].at[pl.ds(rows + start, size)],
            dst_ref=ext[half].at[pl.ds(place + start, size)],
            send_sem=send_sem.at[way, half],
            recv_sem=recv_sem.at[side, half],
            device_id=target,
            device_id_type=MESH,
        )

    def arrival(side, half):
        place = ext[half].at[pl.ds((1 - side) * 2 * rows, rows)]
        return pltpu.make_async_remote_copy(
            src_ref=place,
            dst_ref=place,
            send_sem=send_sem.at[0, half],
            recv_sem=recv_sem.at[side, half],
            device_id=(me, other),
            device_id_type=MESH,
        )

    load(0).wait()
    table_loads[0].wait()
    table_loads[1].wait()

    def transform(i, carry):
        start = pl.multiple_of(i * CHUNK, CHUNK)
        pl.when(i == 1)(load(1).wait)
        re, im = spectra(x_ref, small, forward, start)
        for s, (a, b) in enumerate(whitened(re, im, small)):
            place = s // 8 * 16 + s % 8
            turn[pl.ds(place, CHUNK, stride=PITCH), :] = a
            turn[pl.ds(place + 8, CHUNK, stride=PITCH), :] = b
        part = turn[...].reshape(CHUNK, PITCH, LANES)
        for half in range(2):
            block = part[:, half * 16 : half * 16 + 16]
            ext[half][pl.ds(rows + start, CHUNK)] = block.astype(jnp.bfloat16)

        @pl.when(i == 0)
        def _():
            pl.semaphore_wait(barrier, 3)

        for half in range(2):
            for way in range(2):
                send(way, half, start, CHUNK).start()
        return carry

    lax.fori_loop(0, chunks, transform, 0)

    table_loads[3].wait()
    table_loads[4].wait()
    anchor = me * rows - rows

    def cross(half, into, slot, i):
        one = jnp.clip(members[0, slot] - anchor, 0, 3 * rows - 1)
        two = jnp.clip(members[1, slot] - anchor, 0, 3 * rows - 1)
        a = ext[half][one].astype(jnp.float32)
        b = ext[half][two].astype(jnp.float32)
        ar, ai, br, bi = a[:8], a[8:], b[:8], b[8:]
        place = pl.ds(i, 8, stride=kept)
        into[half, 0, place, :] = ar * br + ai * bi
        into[half, 1, place, :] = ai * br - ar * bi

    def swap(half):
        return pltpu.make_async_remote_copy(
            src_ref=cross_out.at[half],
            dst_ref=cross_in.at[half],
            send_sem=swap_sem.at[0, half],
            recv_sem=swap_sem.at[1, half],
            device_id=(me, other),
            device_id_type=MESH,
        )

    for half in range(2):
        for side in range(2):
            arrival(side, half).wait_recv()
        for i in range(kept):
            cross(half, cross_out, other * kept + i, i)
        swap(half).start()
        for i in range(kept):
            cross(half, cross_own, core * kept + i, i)
    table_loads[2].wait()

    lane = lax.broadcasted_iota(jnp.int32, (kept, 2 * LANES), 1) % LANES
    lags = []
    for half in range(2):
        swap(half).wait()
        both = jnp.concatenate(
            [cross_own[half, i] + cross_in[half, i] for i in range(2)], axis=1
        )
        if half == 0:
            zeroth = both[:kept]
            parts = [
                jnp.where(lane < LANES // 2, 0.0, zeroth),
                both[kept:],
                jnp.where(lane < LANES // 2, zeroth, 0.0),
            ]
            both = jnp.concatenate(parts, axis=0)
        lags.append(dot3(both, inverse))
    lags = jnp.concatenate([lags[0][: 8 * kept], lags[1], lags[0][8 * kept :]], axis=0)
    for part in range(kept // 8):
        bins = []
        for s in range(17):
            place = slice(s * kept + part * 8, s * kept + part * 8 + 8)
            vr, vi = lags[place, :LANES], lags[place, LANES:]
            c, n = small[s : s + 1, :], small[17 + s : 18 + s, :]
            if s == 0:
                bins.append((vr, None))
            elif s == 16:
                bins.append((vr * c - vi * n, None))
            else:
                bins.append((vr * c - vi * n, vr * n + vi * c))
        blocks = real_sum(bins, RADIX, [l1 % RADIX for l1 in range(-8, 8)])
        slot = core * kept + part * 8 + lax.broadcasted_iota(jnp.int32, (8, LANES), 0)
        wanted = slot < live[0]
        for l1 in range(-8, 8):
            out_ref[part * 8 : part * 8 + 8, (l1 + 8) * LANES : (l1 + 9) * LANES] = jnp.where(
                wanted, blocks[l1 % RADIX], 0.0
            )
    for way in range(2):
        for half in range(2):
            send(way, half, 0, rows).wait_send()


def shards(traces, pair_list, live_pairs):
    rows = traces.shape[0]
    kept = rows // 2
    chunks = rows // CHUNK
    forward, inverse, small = tables()
    in_place = functools.partial(pltpu.with_memory_space_constraint, memory_space=pltpu.HBM)
    in_hbm = pl.BlockSpec(memory_space=pltpu.HBM)
    f32, bf16 = jnp.float32, jnp.bfloat16
    return pl.pallas_call(
        functools.partial(kernel, rows),
        out_shape=jax.ShapeDtypeStruct((kept, NLAG), f32),
        in_specs=[in_hbm] * 6,
        out_specs=pl.BlockSpec(memory_space=pltpu.VMEM),
        scratch_shapes=[
            pltpu.SMEM((2, rows), jnp.int32),
            pltpu.SMEM((1,), jnp.int32),
            pltpu.VMEM((rows * RADIX, LANES), f32),
            pltpu.VMEM(forward.shape, bf16),
            pltpu.VMEM(inverse.shape, bf16),
            pltpu.VMEM(small.shape, f32),
            pltpu.VMEM((CHUNK * PITCH, LANES), f32),
            pltpu.VMEM((3 * rows, 16, LANES), bf16),
            pltpu.VMEM((3 * rows, 16, LANES), bf16),
            pltpu.VMEM((2, 2, 8 * kept, LANES), f32),
            pltpu.VMEM((2, 2, 8 * kept, LANES), f32),
            pltpu.VMEM((2, 2, 8 * kept, LANES), f32),
            pltpu.SemaphoreType.DMA((2,)),
            pltpu.SemaphoreType.DMA((5,)),
            pltpu.SemaphoreType.DMA((2, 2)),
            pltpu.SemaphoreType.DMA((2, 2)),
            pltpu.SemaphoreType.DMA((2, 2)),
        ],
        compiler_params=pltpu.CompilerParams(
            collective_id=0, has_side_effects=True, vmem_limit_bytes=32 * 1024 * 1024
        ),
        name="correlate",
    )(
        in_place(traces.reshape(rows * RADIX, LANES)),
        in_place(pair_list.T),
        live_pairs,
        in_place(jnp.asarray(forward)),
        in_place(jnp.asarray(inverse)),
        in_place(jnp.asarray(small)),
    )


def solution(mesh):
    placed = (P("pair", "tm", None), P("pair", None), P("pair"))
    return jax.shard_map(
        shards, mesh=mesh, in_specs=placed, out_specs=P(("pair", "tm"), None), check_vma=False
    )
```

```python
import functools
import math

import jax
import jax.numpy as jnp
import numpy as np
from jax import lax
from jax.experimental import pallas as pl
from jax.experimental.pallas import tpu as pltpu
from jax.sharding import PartitionSpec as P

NT = 4096
FB = 2048
NLAG = 2048
HALF = 64
EPSILON = 1e-06

RADIX = 32
LANES = 128
SLABS = 16
CHUNK = 8
PITCH = 40
MESH = pl.DeviceIdType.MESH


def split(table):
    high = table.astype(jnp.bfloat16)
    low = (table - high.astype(np.float64)).astype(jnp.bfloat16)
    return np.stack([high, low])


def tables():
    n0 = np.arange(LANES)
    k2 = np.arange(LANES // 2)
    q = np.concatenate([k2, LANES - 1 - k2])
    sign = np.concatenate([np.ones(LANES // 2), -np.ones(LANES // 2)])
    angle = 2.0 * math.pi * (n0[:, None] * q[None, :] % LANES) / LANES
    cos, sin = np.cos(angle), np.sin(angle)
    forward = np.block([[cos, -sin * sign], [sin, cos * sign]])
    inverse = np.block([[cos.T, sin.T], [-sin.T * sign[:, None], cos.T * sign[:, None]]])
    inverse = inverse / 64.0
    s = np.arange(SLABS + 1)
    twist = 2.0 * math.pi * (s[:, None] * n0[None, :]) / NT
    k1 = np.stack([np.where(s[:16] == 0, 16, s[:16]), 32 - s[:16]], axis=1)
    index = (k1[:, :, None] - 1 + RADIX * k2[None, None, :]).reshape(SLABS, LANES)
    counted = np.minimum(index + HALF, FB - 1) - np.maximum(index - HALF, 0) + 1
    small = np.zeros((56, LANES))
    small[0:17] = np.cos(twist)
    small[17:34] = np.sin(twist)
    small[34:50] = counted
    return split(forward), split(inverse), small.astype(np.float32)


def scaled(value, factor):
    return value if factor == 1.0 else -value if factor == -1.0 else value * factor


def real_dft(values):
    count = len(values)
    if count == 2:
        return [(values[0] + values[1], None), (values[0] - values[1], None)]
    even, odd = real_dft(values[0::2]), real_dft(values[1::2])
    quarter = count // 4
    bins = [None] * (count // 2 + 1)
    bins[0] = (even[0][0] + odd[0][0], None)
    bins[count // 2] = (even[0][0] - odd[0][0], None)
    for k in range(1, quarter):
        c, s = math.cos(2.0 * math.pi * k / count), math.sin(2.0 * math.pi * k / count)
        (er, ei), (pr, pi) = even[k], odd[k]
        if 8 * k == count:
            tr, ti = (pr + pi) * c, (pi - pr) * c
        else:
            tr, ti = pr * c + pi * s, pi * c - pr * s
        bins[k] = (er + tr, ei + ti)
        bins[count // 2 - k] = (er - tr, ti - ei)
    er, pr = even[quarter][0], odd[quarter][0]
    bins[quarter] = (er, -pr)
    return bins


def real_sum(bins, count, wanted):
    if count == 2:
        (ar, _), (br, _) = bins
        return {l: ar + br if l == 0 else ar - br for l in wanted}
    quarter = count // 4
    even, odd = [], []
    for s in range(quarter):
        (ar, ai), (br, bi) = bins[s], bins[count // 2 - s]
        if s == 0:
            even.append((ar + br, None))
            odd.append((ar - br, None))
            continue
        even.append((ar + br, ai - bi))
        dr, di = ar - br, ai + bi
        c, n = math.cos(2.0 * math.pi * s / count), math.sin(2.0 * math.pi * s / count)
        if 8 * s == count:
            odd.append(((dr - di) * c, (dr + di) * c))
        else:
            odd.append((dr * c - di * n, dr * n + di * c))
    mr, mi = bins[quarter]
    even.append((mr, None))
    odd.append((-mi, None))
    half = count // 2
    from_even = real_sum(even, half, sorted({l // 2 for l in wanted if l % 2 == 0}))
    from_odd = real_sum(odd, half, sorted({l // 2 for l in wanted if l % 2 == 1}))
    return {l: (from_odd if l % 2 else from_even)[l // 2] for l in wanted}


def halves(value):
    high = value.astype(jnp.bfloat16)
    return high, (value - high.astype(jnp.float32)).astype(jnp.bfloat16)


def dot3(value, table):
    high, low = halves(value)
    dot = functools.partial(jnp.dot, preferred_element_type=jnp.float32)
    return dot(high, table[0]) + (dot(low, table[0]) + dot(high, table[1]))


def spectra(x_ref, small, forward, base):
    first = pl.multiple_of(base * PITCH, CHUNK * PITCH)
    values = [x_ref[pl.ds(first + n1, CHUNK, stride=PITCH), :] for n1 in range(RADIX)]
    turned_re, turned_im = [], []
    for s, (re, im) in enumerate(real_dft(values)):
        c, n = small[s : s + 1, :], small[17 + s : 18 + s, :]
        if s == 0:
            turned_re.append(re)
            turned_im.append(jnp.zeros_like(re))
        elif im is None:
            turned_re.append(re * c)
            turned_im.append(-re * n)
        else:
            turned_re.append(re * c + im * n)
            turned_im.append(im * c - re * n)
    rows = jnp.concatenate(
        [jnp.concatenate(turned_re, axis=0), jnp.concatenate(turned_im, axis=0)], axis=1
    )
    final = dot3(rows, forward)
    re = [final[s * CHUNK : (s + 1) * CHUNK, :LANES] for s in range(17)]
    im = [final[s * CHUNK : (s + 1) * CHUNK, LANES:] for s in range(17)]
    first = lax.broadcasted_iota(jnp.int32, (CHUNK, LANES), 1) < LANES // 2
    re[0] = jnp.where(first, re[16], re[0])
    im[0] = jnp.where(first, im[16], im[0])
    return re[:16], im[:16]


def whitened(re, im, small):
    lane = lax.broadcasted_iota(jnp.int32, (CHUNK, LANES), 1)
    first = lane < LANES // 2
    k2 = lane % (LANES // 2)
    size = [jnp.sqrt(a * a + b * b) for a, b in zip(re, im)]
    running = [jnp.zeros_like(size[0])]
    for s in range(1, SLABS):
        running.append(running[-1] + size[s])
    total = running[15] + size[0]
    total = total + pltpu.roll(total, LANES // 2, 1)
    centre = (
        total
        + jnp.where(k2 >= 1, pltpu.roll(total, 1, 1), 0.0)
        + jnp.where(k2 <= 62, pltpu.roll(total, LANES - 1, 1), 0.0)
    )
    before = pltpu.roll(running[15] + size[0], LANES // 2, 1) + running[15]
    out = []
    for s in range(SLABS):
        if s == 0:
            prefix = jnp.where(first, running[15] + size[0], total)
            suffix = jnp.where(first, total - running[15], size[0])
        else:
            prefix = jnp.where(first, running[s], before - running[s - 1])
            suffix = jnp.where(first, total - running[s - 1], running[s] + size[0])
        window = (
            centre
            + jnp.where(k2 >= 2, pltpu.roll(suffix, 2, 1), 0.0)
            + jnp.where(k2 <= 61, pltpu.roll(prefix, LANES - 2, 1), 0.0)
        )
        counted = small[34 + s : 35 + s, :]
        scale = counted / (window + EPSILON * counted)
        out.append((re[s] * scale, im[s] * scale))
    return out


def kernel(
    rows,
    traces,
    pair_list,
    live_pairs,
    forward_hbm,
    inverse_hbm,
    small_hbm,
    out_ref,
    members,
    live,
    x_ref,
    forward,
    inverse,
    small,
    turn,
    ext_0,
    ext_1,
    cross_out,
    cross_own,
    cross_in,
    load_sem,
    table_sem,
    send_sem,
    recv_sem,
    swap_sem,
):
    me = lax.axis_index("pair")
    core = lax.axis_index("tm")
    count = lax.axis_size("pair")
    chunks = rows // CHUNK
    kept = rows // 2
    ext = (ext_0, ext_1)

    def load(channel):
        return pltpu.make_async_copy(
            traces.at[pl.ds(channel * RADIX, RADIX)],
            x_ref.at[pl.ds(channel * PITCH, RADIX)],
            load_sem.at[0 if channel < CHUNK else 1],
        )

    def loaded(i):
        size = CHUNK * RADIX if i == 0 else (rows - CHUNK) * RADIX
        place = x_ref.at[pl.ds(0, size)]
        return pltpu.make_async_copy(traces.at[pl.ds(0, size)], place, load_sem.at[i])

    table_loads = [
        pltpu.make_async_copy(src, dst, table_sem.at[i])
        for i, (src, dst) in enumerate(
            [
                (small_hbm, small),
                (forward_hbm, forward),
                (inverse_hbm, inverse),
                (pair_list, members),
                (live_pairs, live),
            ]
        )
    ]
    first = (me == 0).astype(jnp.int32)
    last = (me == count - 1).astype(jnp.int32)
    other = 1 - core
    ways = (
        ((me - 1 + first, core + first * (other - core)), 2 * rows * (1 - first)),
        ((me + 1 - last, core + last * (other - core)), 2 * rows * last),
    )
    barrier = pltpu.get_barrier_semaphore()
    for target in (ways[0][0], ways[1][0], (me, other)):
        pl.semaphore_signal(barrier, inc=1, device_id=target, device_id_type=MESH)

    for channel in range(CHUNK):
        load(channel).start()
    table_loads[0].start()
    table_loads[1].start()
    for channel in range(CHUNK, rows):
        load(channel).start()
    for copy in table_loads[2:]:
        copy.start()

    def send(way, half, start, size):
        target, place = ways[way]
        return pltpu.make_async_remote_copy(
            src_ref=ext[half].at[pl.ds(rows + start, size)],
            dst_ref=ext[half].at[pl.ds(place + start, size)],
            send_sem=send_sem.at[way],
            recv_sem=recv_sem.at[half],
            device_id=target,
            device_id_type=MESH,
        )

    def sent(way):
        place = ext_0.at[pl.ds(0, 2 * rows)]
        return pltpu.make_async_remote_copy(
            src_ref=place,
            dst_ref=place,
            send_sem=send_sem.at[way],
            recv_sem=recv_sem.at[0],
            device_id=(me, other),
            device_id_type=MESH,
        )

    def arrivals(half):
        place = ext[half].at[pl.ds(0, 2 * rows)]
        return pltpu.make_async_remote_copy(
            src_ref=place,
            dst_ref=place,
            send_sem=send_sem.at[0],
            recv_sem=recv_sem.at[half],
            device_id=(me, other),
            device_id_type=MESH,
        )

    loaded(0).wait()
    table_loads[0].wait()
    table_loads[1].wait()

    def transform(i, carry):
        start = pl.multiple_of(i * CHUNK, CHUNK)
        pl.when(i == 1)(loaded(1).wait)
        re, im = spectra(x_ref, small, forward, start)
        for s, (a, b) in enumerate(whitened(re, im, small)):
            place = s // 8 * 16 + s % 8
            turn[pl.ds(place, CHUNK, stride=PITCH), :] = a
            turn[pl.ds(place + 8, CHUNK, stride=PITCH), :] = b
        part = turn[...].reshape(CHUNK, PITCH, LANES)
        for half in range(2):
            block = part[:, half * 16 : half * 16 + 16]
            ext[half][pl.ds(rows + start, CHUNK)] = block.astype(jnp.bfloat16)

        @pl.when(i == 0)
        def _():
            pl.semaphore_wait(barrier, 3)

        for half in range(2):
            for way in range(2):
                send(way, half, start, CHUNK).start()
        return carry

    lax.fori_loop(0, chunks, transform, 0)

    table_loads[3].wait()
    table_loads[4].wait()
    anchor = me * rows - rows

    def cross(half, into, slot, i):
        one = jnp.clip(members[0, slot] - anchor, 0, 3 * rows - 1)
        two = jnp.clip(members[1, slot] - anchor, 0, 3 * rows - 1)
        a = ext[half][one].astype(jnp.float32)
        b = ext[half][two].astype(jnp.float32)
        ar, ai, br, bi = a[:8], a[8:], b[:8], b[8:]
        place = pl.ds(i, 8, stride=kept)
        into[half, 0, place, :] = ar * br + ai * bi
        into[half, 1, place, :] = ai * br - ar * bi

    def swap(half):
        return pltpu.make_async_remote_copy(
            src_ref=cross_out.at[half],
            dst_ref=cross_in.at[half],
            send_sem=swap_sem.at[0, half],
            recv_sem=swap_sem.at[1, half],
            device_id=(me, other),
            device_id_type=MESH,
        )

    for half in range(2):
        arrivals(half).wait_recv()
        for i in range(kept):
            cross(half, cross_out, other * kept + i, i)
        swap(half).start()
        for i in range(kept):
            cross(half, cross_own, core * kept + i, i)
    table_loads[2].wait()

    lane = lax.broadcasted_iota(jnp.int32, (kept, 2 * LANES), 1) % LANES
    lags = []
    for half in range(2):
        swap(half).wait()
        both = jnp.concatenate(
            [cross_own[half, i] + cross_in[half, i] for i in range(2)], axis=1
        )
        if half == 0:
            zeroth = both[:kept]
            parts = [
                jnp.where(lane < LANES // 2, 0.0, zeroth),
                both[kept:],
                jnp.where(lane < LANES // 2, zeroth, 0.0),
            ]
            both = jnp.concatenate(parts, axis=0)
        lags.append(dot3(both, inverse))
    lags = jnp.concatenate([lags[0][: 8 * kept], lags[1], lags[0][8 * kept :]], axis=0)
    for part in range(kept // 8):
        bins = []
        for s in range(17):
            place = slice(s * kept + part * 8, s * kept + part * 8 + 8)
            vr, vi = lags[place, :LANES], lags[place, LANES:]
            c, n = small[s : s + 1, :], small[17 + s : 18 + s, :]
            if s == 0:
                bins.append((vr, None))
            elif s == 16:
                bins.append((vr * c - vi * n, None))
            else:
                bins.append((vr * c - vi * n, vr * n + vi * c))
        blocks = real_sum(bins, RADIX, [l1 % RADIX for l1 in range(-8, 8)])
        slot = core * kept + part * 8 + lax.broadcasted_iota(jnp.int32, (8, LANES), 0)
        wanted = slot < live[0]
        for l1 in range(-8, 8):
            out_ref[part * 8 : part * 8 + 8, (l1 + 8) * LANES : (l1 + 9) * LANES] = jnp.where(
                wanted, blocks[l1 % RADIX], 0.0
            )
    for way in range(2):
        sent(way).wait_send()


def shards(traces, pair_list, live_pairs):
    rows = traces.shape[0]
    kept = rows // 2
    chunks = rows // CHUNK
    forward, inverse, small = tables()
    in_place = functools.partial(pltpu.with_memory_space_constraint, memory_space=pltpu.HBM)
    in_hbm = pl.BlockSpec(memory_space=pltpu.HBM)
    f32, bf16 = jnp.float32, jnp.bfloat16
    return pl.pallas_call(
        functools.partial(kernel, rows),
        out_shape=jax.ShapeDtypeStruct((kept, NLAG), f32),
        in_specs=[in_hbm] * 6,
        out_specs=pl.BlockSpec(memory_space=pltpu.VMEM),
        scratch_shapes=[
            pltpu.SMEM((2, rows), jnp.int32),
            pltpu.SMEM((1,), jnp.int32),
            pltpu.VMEM((rows * PITCH, LANES), f32),
            pltpu.VMEM(forward.shape, bf16),
            pltpu.VMEM(inverse.shape, bf16),
            pltpu.VMEM(small.shape, f32),
            pltpu.VMEM((CHUNK * PITCH, LANES), f32),
            pltpu.VMEM((3 * rows, 16, LANES), bf16),
            pltpu.VMEM((3 * rows, 16, LANES), bf16),
            pltpu.VMEM((2, 2, 8 * kept, LANES), f32),
            pltpu.VMEM((2, 2, 8 * kept, LANES), f32),
            pltpu.VMEM((2, 2, 8 * kept, LANES), f32),
            pltpu.SemaphoreType.DMA((2,)),
            pltpu.SemaphoreType.DMA((5,)),
            pltpu.SemaphoreType.DMA((2,)),
            pltpu.SemaphoreType.DMA((2,)),
            pltpu.SemaphoreType.DMA((2, 2)),
        ],
        compiler_params=pltpu.CompilerParams(
            collective_id=0, has_side_effects=True, vmem_limit_bytes=32 * 1024 * 1024
        ),
        name="correlate",
    )(
        in_place(traces.reshape(rows * RADIX, LANES)),
        in_place(pair_list.T),
        live_pairs,
        in_place(jnp.asarray(forward)),
        in_place(jnp.asarray(inverse)),
        in_place(jnp.asarray(small)),
    )


def solution(mesh):
    placed = (P("pair", "tm", None), P("pair", None), P("pair"))
    return jax.shard_map(
        shards, mesh=mesh, in_specs=placed, out_specs=P(("pair", "tm"), None), check_vma=False
    )
```

```python
import functools
import math

import jax
import jax.numpy as jnp
import numpy as np
from jax import lax
from jax.experimental import pallas as pl
from jax.experimental.pallas import tpu as pltpu
from jax.sharding import PartitionSpec as P

NT = 4096
FB = 2048
NLAG = 2048
HALF = 64
EPSILON = 1e-06

RADIX = 32
LANES = 128
SLABS = 16
CHUNK = 8
PITCH = 40
MESH = pl.DeviceIdType.MESH


def split(table):
    high = table.astype(jnp.bfloat16)
    low = (table - high.astype(np.float64)).astype(jnp.bfloat16)
    return np.stack([high, low])


def tables():
    n0 = np.arange(LANES)
    k2 = np.arange(LANES // 2)
    q = np.concatenate([k2, LANES - 1 - k2])
    sign = np.concatenate([np.ones(LANES // 2), -np.ones(LANES // 2)])
    angle = 2.0 * math.pi * (n0[:, None] * q[None, :] % LANES) / LANES
    cos, sin = np.cos(angle), np.sin(angle)
    forward = np.block([[cos, -sin * sign], [sin, cos * sign]])
    inverse = np.block([[cos.T, sin.T], [-sin.T * sign[:, None], cos.T * sign[:, None]]])
    inverse = inverse / 64.0
    s = np.arange(SLABS + 1)
    twist = 2.0 * math.pi * (s[:, None] * n0[None, :]) / NT
    k1 = np.stack([np.where(s[:16] == 0, 16, s[:16]), 32 - s[:16]], axis=1)
    index = (k1[:, :, None] - 1 + RADIX * k2[None, None, :]).reshape(SLABS, LANES)
    counted = np.minimum(index + HALF, FB - 1) - np.maximum(index - HALF, 0) + 1
    small = np.zeros((56, LANES))
    small[0:17] = np.cos(twist)
    small[17:34] = np.sin(twist)
    small[34:50] = counted
    return split(forward), split(inverse), small.astype(np.float32)


def scaled(value, factor):
    return value if factor == 1.0 else -value if factor == -1.0 else value * factor


def real_dft(values):
    count = len(values)
    if count == 2:
        return [(values[0] + values[1], None), (values[0] - values[1], None)]
    even, odd = real_dft(values[0::2]), real_dft(values[1::2])
    quarter = count // 4
    bins = [None] * (count // 2 + 1)
    bins[0] = (even[0][0] + odd[0][0], None)
    bins[count // 2] = (even[0][0] - odd[0][0], None)
    for k in range(1, quarter):
        c, s = math.cos(2.0 * math.pi * k / count), math.sin(2.0 * math.pi * k / count)
        (er, ei), (pr, pi) = even[k], odd[k]
        if 8 * k == count:
            tr, ti = (pr + pi) * c, (pi - pr) * c
        else:
            tr, ti = pr * c + pi * s, pi * c - pr * s
        bins[k] = (er + tr, ei + ti)
        bins[count // 2 - k] = (er - tr, ti - ei)
    er, pr = even[quarter][0], odd[quarter][0]
    bins[quarter] = (er, -pr)
    return bins


def real_sum(bins, count, wanted):
    if count == 2:
        (ar, _), (br, _) = bins
        return {l: ar + br if l == 0 else ar - br for l in wanted}
    quarter = count // 4
    even, odd = [], []
    for s in range(quarter):
        (ar, ai), (br, bi) = bins[s], bins[count // 2 - s]
        if s == 0:
            even.append((ar + br, None))
            odd.append((ar - br, None))
            continue
        even.append((ar + br, ai - bi))
        dr, di = ar - br, ai + bi
        c, n = math.cos(2.0 * math.pi * s / count), math.sin(2.0 * math.pi * s / count)
        if 8 * s == count:
            odd.append(((dr - di) * c, (dr + di) * c))
        else:
            odd.append((dr * c - di * n, dr * n + di * c))
    mr, mi = bins[quarter]
    even.append((mr, None))
    odd.append((-mi, None))
    half = count // 2
    from_even = real_sum(even, half, sorted({l // 2 for l in wanted if l % 2 == 0}))
    from_odd = real_sum(odd, half, sorted({l // 2 for l in wanted if l % 2 == 1}))
    return {l: (from_odd if l % 2 else from_even)[l // 2] for l in wanted}


def halves(value):
    high = value.astype(jnp.bfloat16)
    return high, (value - high.astype(jnp.float32)).astype(jnp.bfloat16)


def dot3(value, table):
    high, low = halves(value)
    dot = functools.partial(jnp.dot, preferred_element_type=jnp.float32)
    return dot(high, table[0]) + (dot(low, table[0]) + dot(high, table[1]))


def spectra(x_ref, small, forward, base):
    first = pl.multiple_of(base * PITCH, CHUNK * PITCH)
    values = [x_ref[pl.ds(first + n1, CHUNK, stride=PITCH), :] for n1 in range(RADIX)]
    turned_re, turned_im = [], []
    for s, (re, im) in enumerate(real_dft(values)):
        c, n = small[s : s + 1, :], small[17 + s : 18 + s, :]
        if s == 0:
            turned_re.append(re)
            turned_im.append(jnp.zeros_like(re))
        elif im is None:
            turned_re.append(re * c)
            turned_im.append(-re * n)
        else:
            turned_re.append(re * c + im * n)
            turned_im.append(im * c - re * n)
    rows = jnp.concatenate(
        [jnp.concatenate(turned_re, axis=0), jnp.concatenate(turned_im, axis=0)], axis=1
    )
    final = dot3(rows, forward)
    re = [final[s * CHUNK : (s + 1) * CHUNK, :LANES] for s in range(17)]
    im = [final[s * CHUNK : (s + 1) * CHUNK, LANES:] for s in range(17)]
    first = lax.broadcasted_iota(jnp.int32, (CHUNK, LANES), 1) < LANES // 2
    re[0] = jnp.where(first, re[16], re[0])
    im[0] = jnp.where(first, im[16], im[0])
    return re[:16], im[:16]


def whitened(re, im, small):
    lane = lax.broadcasted_iota(jnp.int32, (CHUNK, LANES), 1)
    first = lane < LANES // 2
    k2 = lane % (LANES // 2)
    size = [jnp.sqrt(a * a + b * b) for a, b in zip(re, im)]
    running = [jnp.zeros_like(size[0])]
    for s in range(1, SLABS):
        running.append(running[-1] + size[s])
    total = running[15] + size[0]
    total = total + pltpu.roll(total, LANES // 2, 1)
    centre = (
        total
        + jnp.where(k2 >= 1, pltpu.roll(total, 1, 1), 0.0)
        + jnp.where(k2 <= 62, pltpu.roll(total, LANES - 1, 1), 0.0)
    )
    before = pltpu.roll(running[15] + size[0], LANES // 2, 1) + running[15]
    out = []
    for s in range(SLABS):
        if s == 0:
            prefix = jnp.where(first, running[15] + size[0], total)
            suffix = jnp.where(first, total - running[15], size[0])
        else:
            prefix = jnp.where(first, running[s], before - running[s - 1])
            suffix = jnp.where(first, total - running[s - 1], running[s] + size[0])
        window = (
            centre
            + jnp.where(k2 >= 2, pltpu.roll(suffix, 2, 1), 0.0)
            + jnp.where(k2 <= 61, pltpu.roll(prefix, LANES - 2, 1), 0.0)
        )
        counted = small[34 + s : 35 + s, :]
        scale = counted / (window + EPSILON * counted)
        out.append((re[s] * scale, im[s] * scale))
    return out


def kernel(
    rows,
    traces,
    pair_list,
    live_pairs,
    forward_hbm,
    inverse_hbm,
    small_hbm,
    out_ref,
    members,
    local,
    live,
    x_ref,
    forward,
    inverse,
    small,
    turn,
    ext_0,
    ext_1,
    cross_out,
    cross_own,
    cross_in,
    load_sem,
    table_sem,
    send_sem,
    recv_sem,
    swap_sem,
):
    me = lax.axis_index("pair")
    core = lax.axis_index("tm")
    count = lax.axis_size("pair")
    chunks = rows // CHUNK
    kept = rows // 2
    ext = (ext_0, ext_1)

    def load(channel):
        return pltpu.make_async_copy(
            traces.at[pl.ds(channel * RADIX, RADIX)],
            x_ref.at[pl.ds(channel * PITCH, RADIX)],
            load_sem.at[0 if channel < CHUNK else 1],
        )

    def loaded(i):
        size = CHUNK * RADIX if i == 0 else (rows - CHUNK) * RADIX
        place = x_ref.at[pl.ds(0, size)]
        return pltpu.make_async_copy(traces.at[pl.ds(0, size)], place, load_sem.at[i])

    table_loads = [
        pltpu.make_async_copy(src, dst, table_sem.at[i])
        for i, (src, dst) in enumerate(
            [
                (small_hbm, small),
                (forward_hbm, forward),
                (inverse_hbm, inverse),
                (pair_list, members),
                (live_pairs, live),
            ]
        )
    ]
    first = (me == 0).astype(jnp.int32)
    last = (me == count - 1).astype(jnp.int32)
    other = 1 - core
    ways = (
        ((me - 1 + first, core + first * (other - core)), 2 * rows * (1 - first)),
        ((me + 1 - last, core + last * (other - core)), 2 * rows * last),
    )
    for channel in range(CHUNK):
        load(channel).start()
    table_loads[0].start()
    table_loads[1].start()
    barrier = pltpu.get_barrier_semaphore()
    for target in (ways[0][0], ways[1][0], (me, other)):
        pl.semaphore_signal(barrier, inc=1, device_id=target, device_id_type=MESH)

    for channel in range(CHUNK, rows):
        load(channel).start()
    for copy in table_loads[2:]:
        copy.start()

    def send(way, half, start, size):
        target, place = ways[way]
        return pltpu.make_async_remote_copy(
            src_ref=ext[half].at[pl.ds(rows + start, size)],
            dst_ref=ext[half].at[pl.ds(place + start, size)],
            send_sem=send_sem.at[way],
            recv_sem=recv_sem.at[half],
            device_id=target,
            device_id_type=MESH,
        )

    def sent(way):
        place = ext_0.at[pl.ds(0, 2 * rows)]
        return pltpu.make_async_remote_copy(
            src_ref=place,
            dst_ref=place,
            send_sem=send_sem.at[way],
            recv_sem=recv_sem.at[0],
            device_id=(me, other),
            device_id_type=MESH,
        )

    def arrivals(half):
        place = ext[half].at[pl.ds(0, 2 * rows)]
        return pltpu.make_async_remote_copy(
            src_ref=place,
            dst_ref=place,
            send_sem=send_sem.at[0],
            recv_sem=recv_sem.at[half],
            device_id=(me, other),
            device_id_type=MESH,
        )

    loaded(0).wait()
    table_loads[0].wait()
    table_loads[1].wait()

    def transform(i, carry):
        start = pl.multiple_of(i * CHUNK, CHUNK)
        pl.when(i == 1)(loaded(1).wait)
        re, im = spectra(x_ref, small, forward, start)
        for s, (a, b) in enumerate(whitened(re, im, small)):
            place = s // 8 * 16 + s % 8
            turn[pl.ds(place, CHUNK, stride=PITCH), :] = a
            turn[pl.ds(place + 8, CHUNK, stride=PITCH), :] = b
        part = turn[...].reshape(CHUNK, PITCH, LANES)
        for half in range(2):
            block = part[:, half * 16 : half * 16 + 16]
            ext[half][pl.ds(rows + start, CHUNK)] = block.astype(jnp.bfloat16)

        @pl.when(i == 0)
        def _():
            pl.semaphore_wait(barrier, 3)

        for half in range(2):
            for way in range(2):
                send(way, half, start, CHUNK).start()
        return carry

    lax.fori_loop(0, chunks, transform, 0)

    table_loads[3].wait()
    table_loads[4].wait()
    anchor = me * rows - rows

    def localise(slot, carry):
        for k in range(2):
            local[k, slot] = jnp.clip(members[k, slot] - anchor, 0, 3 * rows - 1)
        return carry

    lax.fori_loop(0, rows, localise, 0)

    def cross(half, into, slot, i):
        one, two = local[0, slot], local[1, slot]
        a = ext[half][one].astype(jnp.float32)
        b = ext[half][two].astype(jnp.float32)
        ar, ai, br, bi = a[:8], a[8:], b[:8], b[8:]
        place = pl.ds(i, 8, stride=kept)
        into[half, 0, place, :] = ar * br + ai * bi
        into[half, 1, place, :] = ai * br - ar * bi

    def swap(half):
        return pltpu.make_async_remote_copy(
            src_ref=cross_out.at[half],
            dst_ref=cross_in.at[half],
            send_sem=swap_sem.at[0, half],
            recv_sem=swap_sem.at[1, half],
            device_id=(me, other),
            device_id_type=MESH,
        )

    for half in range(2):
        arrivals(half).wait_recv()
        for i in range(kept):
            cross(half, cross_out, other * kept + i, i)
        swap(half).start()
        for i in range(kept):
            cross(half, cross_own, core * kept + i, i)
    table_loads[2].wait()

    lane = lax.broadcasted_iota(jnp.int32, (kept, 2 * LANES), 1) % LANES
    lags = []
    for half in range(2):
        swap(half).wait()
        both = jnp.concatenate(
            [cross_own[half, i] + cross_in[half, i] for i in range(2)], axis=1
        )
        if half == 0:
            zeroth = both[:kept]
            parts = [
                jnp.where(lane < LANES // 2, 0.0, zeroth),
                both[kept:],
                jnp.where(lane < LANES // 2, zeroth, 0.0),
            ]
            both = jnp.concatenate(parts, axis=0)
        lags.append(dot3(both, inverse))
    lags = jnp.concatenate([lags[0][: 8 * kept], lags[1], lags[0][8 * kept :]], axis=0)
    for part in range(kept // 8):
        bins = []
        for s in range(17):
            place = slice(s * kept + part * 8, s * kept + part * 8 + 8)
            vr, vi = lags[place, :LANES], lags[place, LANES:]
            c, n = small[s : s + 1, :], small[17 + s : 18 + s, :]
            if s == 0:
                bins.append((vr, None))
            elif s == 16:
                bins.append((vr * c - vi * n, None))
            else:
                bins.append((vr * c - vi * n, vr * n + vi * c))
        blocks = real_sum(bins, RADIX, [l1 % RADIX for l1 in range(-8, 8)])
        slot = core * kept + part * 8 + lax.broadcasted_iota(jnp.int32, (8, LANES), 0)
        wanted = slot < live[0]
        for l1 in range(-8, 8):
            out_ref[part * 8 : part * 8 + 8, (l1 + 8) * LANES : (l1 + 9) * LANES] = jnp.where(
                wanted, blocks[l1 % RADIX], 0.0
            )
    for way in range(2):
        sent(way).wait_send()


def shards(traces, pair_list, live_pairs):
    rows = traces.shape[0]
    kept = rows // 2
    chunks = rows // CHUNK
    forward, inverse, small = tables()
    in_place = functools.partial(pltpu.with_memory_space_constraint, memory_space=pltpu.HBM)
    in_hbm = pl.BlockSpec(memory_space=pltpu.HBM)
    f32, bf16 = jnp.float32, jnp.bfloat16
    return pl.pallas_call(
        functools.partial(kernel, rows),
        out_shape=jax.ShapeDtypeStruct((kept, NLAG), f32),
        in_specs=[in_hbm] * 6,
        out_specs=pl.BlockSpec(memory_space=pltpu.VMEM),
        scratch_shapes=[
            pltpu.SMEM((2, rows), jnp.int32),
            pltpu.SMEM((2, rows), jnp.int32),
            pltpu.SMEM((1,), jnp.int32),
            pltpu.VMEM((rows * PITCH, LANES), f32),
            pltpu.VMEM(forward.shape, bf16),
            pltpu.VMEM(inverse.shape, bf16),
            pltpu.VMEM(small.shape, f32),
            pltpu.VMEM((CHUNK * PITCH, LANES), f32),
            pltpu.VMEM((3 * rows, 16, LANES), bf16),
            pltpu.VMEM((3 * rows, 16, LANES), bf16),
            pltpu.VMEM((2, 2, 8 * kept, LANES), f32),
            pltpu.VMEM((2, 2, 8 * kept, LANES), f32),
            pltpu.VMEM((2, 2, 8 * kept, LANES), f32),
            pltpu.SemaphoreType.DMA((2,)),
            pltpu.SemaphoreType.DMA((5,)),
            pltpu.SemaphoreType.DMA((2,)),
            pltpu.SemaphoreType.DMA((2,)),
            pltpu.SemaphoreType.DMA((2, 2)),
        ],
        compiler_params=pltpu.CompilerParams(
            collective_id=0, has_side_effects=True, vmem_limit_bytes=32 * 1024 * 1024
        ),
        name="correlate",
    )(
        in_place(traces.reshape(rows * RADIX, LANES)),
        in_place(pair_list.T),
        live_pairs,
        in_place(jnp.asarray(forward)),
        in_place(jnp.asarray(inverse)),
        in_place(jnp.asarray(small)),
    )


def solution(mesh):
    placed = (P("pair", "tm", None), P("pair", None), P("pair"))
    return jax.shard_map(
        shards, mesh=mesh, in_specs=placed, out_specs=P(("pair", "tm"), None), check_vma=False
    )
```

```python
import functools
import math

import jax
import jax.numpy as jnp
import numpy as np
from jax import lax
from jax.experimental import pallas as pl
from jax.experimental.pallas import tpu as pltpu
from jax.sharding import PartitionSpec as P

NT = 4096
FB = 2048
NLAG = 2048
HALF = 64
EPSILON = 1e-06

RADIX = 32
LANES = 128
SLABS = 16
CHUNK = 8
PITCH = 40
MESH = pl.DeviceIdType.MESH


def split(table):
    high = table.astype(jnp.bfloat16)
    low = (table - high.astype(np.float64)).astype(jnp.bfloat16)
    return np.stack([high, low])


def tables():
    n0 = np.arange(LANES)
    k2 = np.arange(LANES // 2)
    q = np.concatenate([k2, LANES - 1 - k2])
    sign = np.concatenate([np.ones(LANES // 2), -np.ones(LANES // 2)])
    angle = 2.0 * math.pi * (n0[:, None] * q[None, :] % LANES) / LANES
    cos, sin = np.cos(angle), np.sin(angle)
    forward = np.block([[cos, -sin * sign], [sin, cos * sign]])
    inverse = np.block([[cos.T, sin.T], [-sin.T * sign[:, None], cos.T * sign[:, None]]])
    inverse = inverse / 64.0
    s = np.arange(SLABS + 1)
    twist = 2.0 * math.pi * (s[:, None] * n0[None, :]) / NT
    k1 = np.stack([np.where(s[:16] == 0, 16, s[:16]), 32 - s[:16]], axis=1)
    index = (k1[:, :, None] - 1 + RADIX * k2[None, None, :]).reshape(SLABS, LANES)
    counted = np.minimum(index + HALF, FB - 1) - np.maximum(index - HALF, 0) + 1
    small = np.zeros((56, LANES))
    small[0:17] = np.cos(twist)
    small[17:34] = np.sin(twist)
    small[34:50] = counted
    return split(forward), split(inverse), small.astype(np.float32)


def scaled(value, factor):
    return value if factor == 1.0 else -value if factor == -1.0 else value * factor


def real_dft(values):
    count = len(values)
    if count == 2:
        return [(values[0] + values[1], None), (values[0] - values[1], None)]
    even, odd = real_dft(values[0::2]), real_dft(values[1::2])
    quarter = count // 4
    bins = [None] * (count // 2 + 1)
    bins[0] = (even[0][0] + odd[0][0], None)
    bins[count // 2] = (even[0][0] - odd[0][0], None)
    for k in range(1, quarter):
        c, s = math.cos(2.0 * math.pi * k / count), math.sin(2.0 * math.pi * k / count)
        (er, ei), (pr, pi) = even[k], odd[k]
        if 8 * k == count:
            tr, ti = (pr + pi) * c, (pi - pr) * c
        else:
            tr, ti = pr * c + pi * s, pi * c - pr * s
        bins[k] = (er + tr, ei + ti)
        bins[count // 2 - k] = (er - tr, ti - ei)
    er, pr = even[quarter][0], odd[quarter][0]
    bins[quarter] = (er, -pr)
    return bins


def real_sum(bins, count, wanted):
    if count == 2:
        (ar, _), (br, _) = bins
        return {l: ar + br if l == 0 else ar - br for l in wanted}
    quarter = count // 4
    even, odd = [], []
    for s in range(quarter):
        (ar, ai), (br, bi) = bins[s], bins[count // 2 - s]
        if s == 0:
            even.append((ar + br, None))
            odd.append((ar - br, None))
            continue
        even.append((ar + br, ai - bi))
        dr, di = ar - br, ai + bi
        c, n = math.cos(2.0 * math.pi * s / count), math.sin(2.0 * math.pi * s / count)
        if 8 * s == count:
            odd.append(((dr - di) * c, (dr + di) * c))
        else:
            odd.append((dr * c - di * n, dr * n + di * c))
    mr, mi = bins[quarter]
    even.append((mr, None))
    odd.append((-mi, None))
    half = count // 2
    from_even = real_sum(even, half, sorted({l // 2 for l in wanted if l % 2 == 0}))
    from_odd = real_sum(odd, half, sorted({l // 2 for l in wanted if l % 2 == 1}))
    return {l: (from_odd if l % 2 else from_even)[l // 2] for l in wanted}


def halves(value):
    high = value.astype(jnp.bfloat16)
    return high, (value - high.astype(jnp.float32)).astype(jnp.bfloat16)


def dot3(value, table):
    high, low = halves(value)
    dot = functools.partial(jnp.dot, preferred_element_type=jnp.float32)
    depth = jnp.concatenate([table[0], table[1]], axis=0)
    return dot(jnp.concatenate([high, high], axis=1), depth) + dot(low, table[0])


def spectra(x_ref, small, forward, base):
    first = pl.multiple_of(base * PITCH, CHUNK * PITCH)
    values = [x_ref[pl.ds(first + n1, CHUNK, stride=PITCH), :] for n1 in range(RADIX)]
    turned_re, turned_im = [], []
    for s, (re, im) in enumerate(real_dft(values)):
        c, n = small[s : s + 1, :], small[17 + s : 18 + s, :]
        if s == 0:
            turned_re.append(re)
            turned_im.append(jnp.zeros_like(re))
        elif im is None:
            turned_re.append(re * c)
            turned_im.append(-re * n)
        else:
            turned_re.append(re * c + im * n)
            turned_im.append(im * c - re * n)
    rows = jnp.concatenate(
        [jnp.concatenate(turned_re, axis=0), jnp.concatenate(turned_im, axis=0)], axis=1
    )
    final = dot3(rows, forward)
    re = [final[s * CHUNK : (s + 1) * CHUNK, :LANES] for s in range(17)]
    im = [final[s * CHUNK : (s + 1) * CHUNK, LANES:] for s in range(17)]
    first = lax.broadcasted_iota(jnp.int32, (CHUNK, LANES), 1) < LANES // 2
    re[0] = jnp.where(first, re[16], re[0])
    im[0] = jnp.where(first, im[16], im[0])
    return re[:16], im[:16]


def whitened(re, im, small):
    lane = lax.broadcasted_iota(jnp.int32, (CHUNK, LANES), 1)
    first = lane < LANES // 2
    k2 = lane % (LANES // 2)
    size = [jnp.sqrt(a * a + b * b) for a, b in zip(re, im)]
    running = [jnp.zeros_like(size[0])]
    for s in range(1, SLABS):
        running.append(running[-1] + size[s])
    total = running[15] + size[0]
    total = total + pltpu.roll(total, LANES // 2, 1)
    centre = (
        total
        + jnp.where(k2 >= 1, pltpu.roll(total, 1, 1), 0.0)
        + jnp.where(k2 <= 62, pltpu.roll(total, LANES - 1, 1), 0.0)
    )
    before = pltpu.roll(running[15] + size[0], LANES // 2, 1) + running[15]
    out = []
    for s in range(SLABS):
        if s == 0:
            prefix = jnp.where(first, running[15] + size[0], total)
            suffix = jnp.where(first, total - running[15], size[0])
        else:
            prefix = jnp.where(first, running[s], before - running[s - 1])
            suffix = jnp.where(first, total - running[s - 1], running[s] + size[0])
        window = (
            centre
            + jnp.where(k2 >= 2, pltpu.roll(suffix, 2, 1), 0.0)
            + jnp.where(k2 <= 61, pltpu.roll(prefix, LANES - 2, 1), 0.0)
        )
        counted = small[34 + s : 35 + s, :]
        scale = counted / (window + EPSILON * counted)
        out.append((re[s] * scale, im[s] * scale))
    return out


def kernel(
    rows,
    traces,
    pair_list,
    live_pairs,
    forward_hbm,
    inverse_hbm,
    small_hbm,
    out_ref,
    members,
    local,
    live,
    x_ref,
    forward,
    inverse,
    small,
    turn,
    ext_0,
    ext_1,
    cross_out,
    cross_own,
    cross_in,
    load_sem,
    table_sem,
    send_sem,
    recv_sem,
    swap_sem,
):
    me = lax.axis_index("pair")
    core = lax.axis_index("tm")
    count = lax.axis_size("pair")
    chunks = rows // CHUNK
    kept = rows // 2
    ext = (ext_0, ext_1)

    def load(channel):
        return pltpu.make_async_copy(
            traces.at[pl.ds(channel * RADIX, RADIX)],
            x_ref.at[pl.ds(channel * PITCH, RADIX)],
            load_sem.at[0 if channel < CHUNK else 1],
        )

    def loaded(i):
        size = CHUNK * RADIX if i == 0 else (rows - CHUNK) * RADIX
        place = x_ref.at[pl.ds(0, size)]
        return pltpu.make_async_copy(traces.at[pl.ds(0, size)], place, load_sem.at[i])

    table_loads = [
        pltpu.make_async_copy(src, dst, table_sem.at[i])
        for i, (src, dst) in enumerate(
            [
                (small_hbm, small),
                (forward_hbm, forward),
                (inverse_hbm, inverse),
                (pair_list, members),
                (live_pairs, live),
            ]
        )
    ]
    first = (me == 0).astype(jnp.int32)
    last = (me == count - 1).astype(jnp.int32)
    other = 1 - core
    ways = (
        ((me - 1 + first, core + first * (other - core)), 2 * rows * (1 - first)),
        ((me + 1 - last, core + last * (other - core)), 2 * rows * last),
    )
    for channel in range(CHUNK):
        load(channel).start()
    table_loads[0].start()
    table_loads[1].start()
    barrier = pltpu.get_barrier_semaphore()
    for target in (ways[0][0], ways[1][0], (me, other)):
        pl.semaphore_signal(barrier, inc=1, device_id=target, device_id_type=MESH)

    for channel in range(CHUNK, rows):
        load(channel).start()

    def send(way, half, start, size):
        target, place = ways[way]
        return pltpu.make_async_remote_copy(
            src_ref=ext[half].at[pl.ds(rows + start, size)],
            dst_ref=ext[half].at[pl.ds(place + start, size)],
            send_sem=send_sem.at[way],
            recv_sem=recv_sem.at[half],
            device_id=target,
            device_id_type=MESH,
        )

    def sent(way):
        place = ext_0.at[pl.ds(0, 2 * rows)]
        return pltpu.make_async_remote_copy(
            src_ref=place,
            dst_ref=place,
            send_sem=send_sem.at[way],
            recv_sem=recv_sem.at[0],
            device_id=(me, other),
            device_id_type=MESH,
        )

    def arrivals(half):
        place = ext[half].at[pl.ds(0, 2 * rows)]
        return pltpu.make_async_remote_copy(
            src_ref=place,
            dst_ref=place,
            send_sem=send_sem.at[0],
            recv_sem=recv_sem.at[half],
            device_id=(me, other),
            device_id_type=MESH,
        )

    loaded(0).wait()
    table_loads[0].wait()
    table_loads[1].wait()
    for copy in table_loads[2:]:
        copy.start()

    def transform(i, carry):
        start = pl.multiple_of(i * CHUNK, CHUNK)
        pl.when(i == 1)(loaded(1).wait)
        re, im = spectra(x_ref, small, forward, start)
        for s, (a, b) in enumerate(whitened(re, im, small)):
            place = s // 8 * 16 + s % 8
            turn[pl.ds(place, CHUNK, stride=PITCH), :] = a
            turn[pl.ds(place + 8, CHUNK, stride=PITCH), :] = b
        part = turn[...].reshape(CHUNK, PITCH, LANES)
        for half in range(2):
            block = part[:, half * 16 : half * 16 + 16]
            ext[half][pl.ds(rows + start, CHUNK)] = block.astype(jnp.bfloat16)

        @pl.when(i == 0)
        def _():
            pl.semaphore_wait(barrier, 3)

        for half in range(2):
            for way in range(2):
                send(way, half, start, CHUNK).start()
        return carry

    lax.fori_loop(0, chunks, transform, 0)

    table_loads[3].wait()
    table_loads[4].wait()
    anchor = me * rows - rows

    def localise(slot, carry):
        for k in range(2):
            local[k, slot] = jnp.clip(members[k, slot] - anchor, 0, 3 * rows - 1)
        return carry

    lax.fori_loop(0, rows, localise, 0)

    def cross(half, into, slot, i):
        one, two = local[0, slot], local[1, slot]
        a = ext[half][one].astype(jnp.float32)
        b = ext[half][two].astype(jnp.float32)
        ar, ai, br, bi = a[:8], a[8:], b[:8], b[8:]
        place = pl.ds(i, 8, stride=kept)
        into[half, 0, place, :] = ar * br + ai * bi
        into[half, 1, place, :] = ai * br - ar * bi

    def swap(half):
        return pltpu.make_async_remote_copy(
            src_ref=cross_out.at[half],
            dst_ref=cross_in.at[half],
            send_sem=swap_sem.at[0, half],
            recv_sem=swap_sem.at[1, half],
            device_id=(me, other),
            device_id_type=MESH,
        )

    for half in range(2):
        arrivals(half).wait_recv()
        for i in range(kept):
            cross(half, cross_out, other * kept + i, i)
        swap(half).start()
        for i in range(kept):
            cross(half, cross_own, core * kept + i, i)
    table_loads[2].wait()

    lane = lax.broadcasted_iota(jnp.int32, (kept, 2 * LANES), 1) % LANES
    lags = []
    for half in range(2):
        swap(half).wait()
        both = jnp.concatenate(
            [cross_own[half, i] + cross_in[half, i] for i in range(2)], axis=1
        )
        if half == 0:
            zeroth = both[:kept]
            parts = [
                jnp.where(lane < LANES // 2, 0.0, zeroth),
                both[kept:],
                jnp.where(lane < LANES // 2, zeroth, 0.0),
            ]
            both = jnp.concatenate(parts, axis=0)
        lags.append(dot3(both, inverse))
    lags = jnp.concatenate([lags[0][: 8 * kept], lags[1], lags[0][8 * kept :]], axis=0)
    for part in range(kept // 8):
        bins = []
        for s in range(17):
            place = slice(s * kept + part * 8, s * kept + part * 8 + 8)
            vr, vi = lags[place, :LANES], lags[place, LANES:]
            c, n = small[s : s + 1, :], small[17 + s : 18 + s, :]
            if s == 0:
                bins.append((vr, None))
            elif s == 16:
                bins.append((vr * c - vi * n, None))
            else:
                bins.append((vr * c - vi * n, vr * n + vi * c))
        blocks = real_sum(bins, RADIX, [l1 % RADIX for l1 in range(-8, 8)])
        slot = core * kept + part * 8 + lax.broadcasted_iota(jnp.int32, (8, LANES), 0)
        wanted = slot < live[0]
        for l1 in range(-8, 8):
            out_ref[part * 8 : part * 8 + 8, (l1 + 8) * LANES : (l1 + 9) * LANES] = jnp.where(
                wanted, blocks[l1 % RADIX], 0.0
            )
    for way in range(2):
        sent(way).wait_send()


def shards(traces, pair_list, live_pairs):
    rows = traces.shape[0]
    kept = rows // 2
    chunks = rows // CHUNK
    forward, inverse, small = tables()
    in_place = functools.partial(pltpu.with_memory_space_constraint, memory_space=pltpu.HBM)
    in_hbm = pl.BlockSpec(memory_space=pltpu.HBM)
    f32, bf16 = jnp.float32, jnp.bfloat16
    return pl.pallas_call(
        functools.partial(kernel, rows),
        out_shape=jax.ShapeDtypeStruct((kept, NLAG), f32),
        in_specs=[in_hbm] * 6,
        out_specs=pl.BlockSpec(memory_space=pltpu.VMEM),
        scratch_shapes=[
            pltpu.SMEM((2, rows), jnp.int32),
            pltpu.SMEM((2, rows), jnp.int32),
            pltpu.SMEM((1,), jnp.int32),
            pltpu.VMEM((rows * PITCH, LANES), f32),
            pltpu.VMEM(forward.shape, bf16),
            pltpu.VMEM(inverse.shape, bf16),
            pltpu.VMEM(small.shape, f32),
            pltpu.VMEM((CHUNK * PITCH, LANES), f32),
            pltpu.VMEM((3 * rows, 16, LANES), bf16),
            pltpu.VMEM((3 * rows, 16, LANES), bf16),
            pltpu.VMEM((2, 2, 8 * kept, LANES), f32),
            pltpu.VMEM((2, 2, 8 * kept, LANES), f32),
            pltpu.VMEM((2, 2, 8 * kept, LANES), f32),
            pltpu.SemaphoreType.DMA((2,)),
            pltpu.SemaphoreType.DMA((5,)),
            pltpu.SemaphoreType.DMA((2,)),
            pltpu.SemaphoreType.DMA((2,)),
            pltpu.SemaphoreType.DMA((2, 2)),
        ],
        compiler_params=pltpu.CompilerParams(
            collective_id=0, has_side_effects=True, vmem_limit_bytes=32 * 1024 * 1024
        ),
        name="correlate",
    )(
        in_place(traces.reshape(rows * RADIX, LANES)),
        in_place(pair_list.T),
        live_pairs,
        in_place(jnp.asarray(forward)),
        in_place(jnp.asarray(inverse)),
        in_place(jnp.asarray(small)),
    )


def solution(mesh):
    placed = (P("pair", "tm", None), P("pair", None), P("pair"))
    return jax.shard_map(
        shards, mesh=mesh, in_specs=placed, out_specs=P(("pair", "tm"), None), check_vma=False
    )
```

```python
import functools
import math

import jax
import jax.numpy as jnp
import numpy as np
from jax import lax
from jax.experimental import pallas as pl
from jax.experimental.pallas import tpu as pltpu
from jax.sharding import PartitionSpec as P

NT = 4096
FB = 2048
NLAG = 2048
HALF = 64
EPSILON = 1e-06

RADIX = 32
LANES = 128
SLABS = 16
CHUNK = 8
PITCH = 40
MESH = pl.DeviceIdType.MESH


def split(table):
    high = table.astype(jnp.bfloat16)
    low = (table - high.astype(np.float64)).astype(jnp.bfloat16)
    return np.stack([high, low])


def tables():
    n0 = np.arange(LANES)
    k2 = np.arange(LANES // 2)
    q = np.concatenate([k2, LANES - 1 - k2])
    sign = np.concatenate([np.ones(LANES // 2), -np.ones(LANES // 2)])
    angle = 2.0 * math.pi * (n0[:, None] * q[None, :] % LANES) / LANES
    cos, sin = np.cos(angle), np.sin(angle)
    forward = np.block([[cos, -sin * sign], [sin, cos * sign]])
    inverse = np.block([[cos.T, sin.T], [-sin.T * sign[:, None], cos.T * sign[:, None]]])
    inverse = inverse / 64.0
    s = np.arange(SLABS + 1)
    twist = 2.0 * math.pi * (s[:, None] * n0[None, :]) / NT
    k1 = np.stack([np.where(s[:16] == 0, 16, s[:16]), 32 - s[:16]], axis=1)
    index = (k1[:, :, None] - 1 + RADIX * k2[None, None, :]).reshape(SLABS, LANES)
    counted = np.minimum(index + HALF, FB - 1) - np.maximum(index - HALF, 0) + 1
    small = np.zeros((56, LANES))
    small[0:17] = np.cos(twist)
    small[17:34] = np.sin(twist)
    small[34:50] = counted
    return split(forward), split(inverse), small.astype(np.float32)


def scaled(value, factor):
    return value if factor == 1.0 else -value if factor == -1.0 else value * factor


def real_dft(values):
    count = len(values)
    if count == 2:
        return [(values[0] + values[1], None), (values[0] - values[1], None)]
    even, odd = real_dft(values[0::2]), real_dft(values[1::2])
    quarter = count // 4
    bins = [None] * (count // 2 + 1)
    bins[0] = (even[0][0] + odd[0][0], None)
    bins[count // 2] = (even[0][0] - odd[0][0], None)
    for k in range(1, quarter):
        c, s = math.cos(2.0 * math.pi * k / count), math.sin(2.0 * math.pi * k / count)
        (er, ei), (pr, pi) = even[k], odd[k]
        if 8 * k == count:
            tr, ti = (pr + pi) * c, (pi - pr) * c
        else:
            tr, ti = pr * c + pi * s, pi * c - pr * s
        bins[k] = (er + tr, ei + ti)
        bins[count // 2 - k] = (er - tr, ti - ei)
    er, pr = even[quarter][0], odd[quarter][0]
    bins[quarter] = (er, -pr)
    return bins


def real_sum(bins, count, wanted):
    if count == 2:
        (ar, _), (br, _) = bins
        return {l: ar + br if l == 0 else ar - br for l in wanted}
    quarter = count // 4
    even, odd = [], []
    for s in range(quarter):
        (ar, ai), (br, bi) = bins[s], bins[count // 2 - s]
        if s == 0:
            even.append((ar + br, None))
            odd.append((ar - br, None))
            continue
        even.append((ar + br, ai - bi))
        dr, di = ar - br, ai + bi
        c, n = math.cos(2.0 * math.pi * s / count), math.sin(2.0 * math.pi * s / count)
        if 8 * s == count:
            odd.append(((dr - di) * c, (dr + di) * c))
        else:
            odd.append((dr * c - di * n, dr * n + di * c))
    mr, mi = bins[quarter]
    even.append((mr, None))
    odd.append((-mi, None))
    half = count // 2
    from_even = real_sum(even, half, sorted({l // 2 for l in wanted if l % 2 == 0}))
    from_odd = real_sum(odd, half, sorted({l // 2 for l in wanted if l % 2 == 1}))
    return {l: (from_odd if l % 2 else from_even)[l // 2] for l in wanted}


def halves(value):
    high = value.astype(jnp.bfloat16)
    return high, (value - high.astype(jnp.float32)).astype(jnp.bfloat16)


def dot3(value, table):
    high, low = halves(value)
    dot = functools.partial(jnp.dot, preferred_element_type=jnp.float32)
    return dot(high, table[0]) + (dot(low, table[0]) + dot(high, table[1]))


def spectra(x_ref, small, forward, base):
    first = pl.multiple_of(base * PITCH, CHUNK * PITCH)
    values = [x_ref[pl.ds(first + n1, CHUNK, stride=PITCH), :] for n1 in range(RADIX)]
    turned_re, turned_im = [], []
    for s, (re, im) in enumerate(real_dft(values)):
        c, n = small[s : s + 1, :], small[17 + s : 18 + s, :]
        if s == 0:
            turned_re.append(re)
            turned_im.append(jnp.zeros_like(re))
        elif im is None:
            turned_re.append(re * c)
            turned_im.append(-re * n)
        else:
            turned_re.append(re * c + im * n)
            turned_im.append(im * c - re * n)
    rows = jnp.concatenate(
        [jnp.concatenate(turned_re, axis=0), jnp.concatenate(turned_im, axis=0)], axis=1
    )
    final = dot3(rows, forward)
    re = [final[s * CHUNK : (s + 1) * CHUNK, :LANES] for s in range(17)]
    im = [final[s * CHUNK : (s + 1) * CHUNK, LANES:] for s in range(17)]
    first = lax.broadcasted_iota(jnp.int32, (CHUNK, LANES), 1) < LANES // 2
    re[0] = jnp.where(first, re[16], re[0])
    im[0] = jnp.where(first, im[16], im[0])
    return re[:16], im[:16]


def whitened(re, im, small):
    lane = lax.broadcasted_iota(jnp.int32, (CHUNK, LANES), 1)
    first = lane < LANES // 2
    k2 = lane % (LANES // 2)
    size = [jnp.sqrt(a * a + b * b) for a, b in zip(re, im)]
    running = [jnp.zeros_like(size[0])]
    for s in range(1, SLABS):
        running.append(running[-1] + size[s])
    total = running[15] + size[0]
    total = total + pltpu.roll(total, LANES // 2, 1)
    centre = (
        total
        + jnp.where(k2 >= 1, pltpu.roll(total, 1, 1), 0.0)
        + jnp.where(k2 <= 62, pltpu.roll(total, LANES - 1, 1), 0.0)
    )
    before = pltpu.roll(running[15] + size[0], LANES // 2, 1) + running[15]
    out = []
    for s in range(SLABS):
        if s == 0:
            prefix = jnp.where(first, running[15] + size[0], total)
            suffix = jnp.where(first, total - running[15], size[0])
        else:
            prefix = jnp.where(first, running[s], before - running[s - 1])
            suffix = jnp.where(first, total - running[s - 1], running[s] + size[0])
        window = (
            centre
            + jnp.where(k2 >= 2, pltpu.roll(suffix, 2, 1), 0.0)
            + jnp.where(k2 <= 61, pltpu.roll(prefix, LANES - 2, 1), 0.0)
        )
        counted = small[34 + s : 35 + s, :]
        scale = counted / (window + EPSILON * counted)
        out.append((re[s] * scale, im[s] * scale))
    return out


def kernel(
    rows,
    traces,
    pair_list,
    live_pairs,
    forward_hbm,
    inverse_hbm,
    small_hbm,
    out_ref,
    members,
    local,
    live,
    x_ref,
    forward,
    inverse,
    small,
    turn,
    ext_0,
    ext_1,
    cross_out,
    cross_own,
    cross_in,
    load_sem,
    table_sem,
    send_sem,
    recv_sem,
    swap_sem,
):
    me = lax.axis_index("pair")
    core = lax.axis_index("tm")
    count = lax.axis_size("pair")
    chunks = rows // CHUNK
    kept = rows // 2
    ext = (ext_0, ext_1)

    def load(channel):
        return pltpu.make_async_copy(
            traces.at[pl.ds(channel * RADIX, RADIX)],
            x_ref.at[pl.ds(channel * PITCH, RADIX)],
            load_sem.at[0 if channel < CHUNK else 1],
        )

    def loaded(i):
        size = CHUNK * RADIX if i == 0 else (rows - CHUNK) * RADIX
        place = x_ref.at[pl.ds(0, size)]
        return pltpu.make_async_copy(traces.at[pl.ds(0, size)], place, load_sem.at[i])

    table_loads = [
        pltpu.make_async_copy(src, dst, table_sem.at[i])
        for i, (src, dst) in enumerate(
            [
                (small_hbm, small),
                (forward_hbm, forward),
                (inverse_hbm, inverse),
                (pair_list, members),
                (live_pairs, live),
            ]
        )
    ]
    first = (me == 0).astype(jnp.int32)
    last = (me == count - 1).astype(jnp.int32)
    other = 1 - core
    ways = (
        ((me - 1 + first, core + first * (other - core)), 2 * rows * (1 - first)),
        ((me + 1 - last, core + last * (other - core)), 2 * rows * last),
    )
    for channel in range(CHUNK):
        load(channel).start()
    table_loads[0].start()
    table_loads[1].start()
    barrier = pltpu.get_barrier_semaphore()
    for target in (ways[0][0], ways[1][0], (me, other)):
        pl.semaphore_signal(barrier, inc=1, device_id=target, device_id_type=MESH)

    for channel in range(CHUNK, rows):
        load(channel).start()

    def send(way, half, start, size):
        target, place = ways[way]
        return pltpu.make_async_remote_copy(
            src_ref=ext[half].at[pl.ds(rows + start, size)],
            dst_ref=ext[half].at[pl.ds(place + start, size)],
            send_sem=send_sem.at[way],
            recv_sem=recv_sem.at[half],
            device_id=target,
            device_id_type=MESH,
        )

    def sent(way):
        place = ext_0.at[pl.ds(0, 2 * rows)]
        return pltpu.make_async_remote_copy(
            src_ref=place,
            dst_ref=place,
            send_sem=send_sem.at[way],
            recv_sem=recv_sem.at[0],
            device_id=(me, other),
            device_id_type=MESH,
        )

    def arrivals(half):
        place = ext[half].at[pl.ds(0, 2 * rows)]
        return pltpu.make_async_remote_copy(
            src_ref=place,
            dst_ref=place,
            send_sem=send_sem.at[0],
            recv_sem=recv_sem.at[half],
            device_id=(me, other),
            device_id_type=MESH,
        )

    loaded(0).wait()
    table_loads[0].wait()
    table_loads[1].wait()
    for copy in table_loads[2:]:
        copy.start()

    def transform(i, carry):
        start = pl.multiple_of(i * CHUNK, CHUNK)
        pl.when(i == 1)(loaded(1).wait)
        re, im = spectra(x_ref, small, forward, start)
        for s, (a, b) in enumerate(whitened(re, im, small)):
            place = s // 8 * 16 + s % 8
            turn[pl.ds(place, CHUNK, stride=PITCH), :] = a
            turn[pl.ds(place + 8, CHUNK, stride=PITCH), :] = b
        part = turn[...].reshape(CHUNK, PITCH, LANES)
        for half in range(2):
            block = part[:, half * 16 : half * 16 + 16]
            ext[half][pl.ds(rows + start, CHUNK)] = block.astype(jnp.bfloat16)

        @pl.when(i == 0)
        def _():
            pl.semaphore_wait(barrier, 3)

        for half in range(2):
            for way in range(2):
                send(way, half, start, CHUNK).start()
        return carry

    lax.fori_loop(0, chunks, transform, 0)

    table_loads[3].wait()
    table_loads[4].wait()
    anchor = me * rows - rows

    def localise(slot, carry):
        for k in range(2):
            local[k, slot] = jnp.clip(members[k, slot] - anchor, 0, 3 * rows - 1)
        return carry

    lax.fori_loop(0, rows, localise, 0)

    def cross(half, into, slot, i):
        one, two = local[0, slot], local[1, slot]
        a = ext[half][one].astype(jnp.float32)
        b = ext[half][two].astype(jnp.float32)
        ar, ai, br, bi = a[:8], a[8:], b[:8], b[8:]
        place = pl.ds(i, 8, stride=kept)
        into[half, 0, place, :] = ar * br + ai * bi
        into[half, 1, place, :] = ai * br - ar * bi

    def swap(half):
        return pltpu.make_async_remote_copy(
            src_ref=cross_out.at[half],
            dst_ref=cross_in.at[half],
            send_sem=swap_sem.at[0, half],
            recv_sem=swap_sem.at[1, half],
            device_id=(me, other),
            device_id_type=MESH,
        )

    for half in range(2):
        arrivals(half).wait_recv()
        for i in range(kept):
            cross(half, cross_out, other * kept + i, i)
        swap(half).start()
        for i in range(kept):
            cross(half, cross_own, core * kept + i, i)
    table_loads[2].wait()

    lane = lax.broadcasted_iota(jnp.int32, (kept, 2 * LANES), 1) % LANES
    lags = []
    for half in range(2):
        swap(half).wait()
        both = jnp.concatenate(
            [cross_own[half, i] + cross_in[half, i] for i in range(2)], axis=1
        )
        if half == 0:
            zeroth = both[:kept]
            parts = [
                jnp.where(lane < LANES // 2, 0.0, zeroth),
                both[kept:],
                jnp.where(lane < LANES // 2, zeroth, 0.0),
            ]
            both = jnp.concatenate(parts, axis=0)
        lags.append(dot3(both, inverse))
    lags = jnp.concatenate([lags[0][: 8 * kept], lags[1], lags[0][8 * kept :]], axis=0)
    for part in range(kept // 8):
        bins = []
        for s in range(17):
            place = slice(s * kept + part * 8, s * kept + part * 8 + 8)
            vr, vi = lags[place, :LANES], lags[place, LANES:]
            c, n = small[s : s + 1, :], small[17 + s : 18 + s, :]
            if s == 0:
                bins.append((vr, None))
            elif s == 16:
                bins.append((vr * c - vi * n, None))
            else:
                bins.append((vr * c - vi * n, vr * n + vi * c))
        blocks = real_sum(bins, RADIX, [l1 % RADIX for l1 in range(-8, 8)])
        slot = core * kept + part * 8 + lax.broadcasted_iota(jnp.int32, (8, LANES), 0)
        wanted = slot < live[0]
        for l1 in range(-8, 8):
            out_ref[part * 8 : part * 8 + 8, (l1 + 8) * LANES : (l1 + 9) * LANES] = jnp.where(
                wanted, blocks[l1 % RADIX], 0.0
            )
    for way in range(2):
        sent(way).wait_send()


def shards(traces, pair_list, live_pairs):
    rows = traces.shape[0]
    kept = rows // 2
    chunks = rows // CHUNK
    forward, inverse, small = tables()
    in_place = functools.partial(pltpu.with_memory_space_constraint, memory_space=pltpu.HBM)
    in_hbm = pl.BlockSpec(memory_space=pltpu.HBM)
    f32, bf16 = jnp.float32, jnp.bfloat16
    return pl.pallas_call(
        functools.partial(kernel, rows),
        out_shape=jax.ShapeDtypeStruct((kept, NLAG), f32),
        in_specs=[in_hbm] * 6,
        out_specs=pl.BlockSpec(memory_space=pltpu.VMEM),
        scratch_shapes=[
            pltpu.SMEM((2, rows), jnp.int32),
            pltpu.SMEM((2, rows), jnp.int32),
            pltpu.SMEM((1,), jnp.int32),
            pltpu.VMEM((rows * PITCH, LANES), f32),
            pltpu.VMEM(forward.shape, bf16),
            pltpu.VMEM(inverse.shape, bf16),
            pltpu.VMEM(small.shape, f32),
            pltpu.VMEM((CHUNK * PITCH, LANES), f32),
            pltpu.VMEM((3 * rows, 16, LANES), bf16),
            pltpu.VMEM((3 * rows, 16, LANES), bf16),
            pltpu.VMEM((2, 2, 8 * kept, LANES), f32),
            pltpu.VMEM((2, 2, 8 * kept, LANES), f32),
            pltpu.VMEM((2, 2, 8 * kept, LANES), f32),
            pltpu.SemaphoreType.DMA((2,)),
            pltpu.SemaphoreType.DMA((5,)),
            pltpu.SemaphoreType.DMA((2,)),
            pltpu.SemaphoreType.DMA((2,)),
            pltpu.SemaphoreType.DMA((2, 2)),
        ],
        compiler_params=pltpu.CompilerParams(
            collective_id=0, has_side_effects=True, vmem_limit_bytes=32 * 1024 * 1024
        ),
        name="correlate",
    )(
        in_place(traces.reshape(rows * RADIX, LANES)),
        in_place(pair_list.T),
        live_pairs,
        in_place(jnp.asarray(forward)),
        in_place(jnp.asarray(inverse)),
        in_place(jnp.asarray(small)),
    )


def solution(mesh):
    placed = (P("pair", "tm", None), P("pair", None), P("pair"))
    return jax.shard_map(
        shards, mesh=mesh, in_specs=placed, out_specs=P(("pair", "tm"), None), check_vma=False
    )
```
